256 devices in a mesh: ctx: 64 (over z, y, core), tsp: 4 (over x).
Axes of the slice: x: 4, y: 4, z: 8, core: 2. Of those that a mesh axis runs over, the one named last changes fastest.
Arguments:
- queries: bfloat16 [32768, 5120], P(('ctx', 'tsp')), may hold values from -6 to 6
- keys: bfloat16 [32768, 5120], P(('ctx', 'tsp')), may hold values from -6 to 6
- values: bfloat16 [32768, 5120], P(('ctx', 'tsp')), may hold values from -6 to 6
- cotangent: bfloat16 [32768, 5120], P(('ctx', 'tsp')), may hold values from -6 to 6
- content_bias: float32 [40, 128], P('tsp'), may hold values from -5 to 5
- memory_lengths: int32 [64], P('ctx'), may hold values from 0 to 1536, as said below
- segment_ends: int32 [64], P('ctx'), may hold values from 1 to 512, as said below
Outputs:
- attended: bfloat16 [32768, 5120], P(('ctx', 'tsp'))
- grad_queries: bfloat16 [32768, 5120], P(('ctx', 'tsp'))
- grad_keys: bfloat16 [32768, 5120], P(('ctx', 'tsp'))
- grad_values: bfloat16 [32768, 5120], P(('ctx', 'tsp'))
- grad_bias: float32 [40, 128], P('tsp')
The draws below stay inside these ranges and needn't reach their ends.
Inputs may be any that keep to these rules, and one draw needn't show every extreme that they name: memory_lengths[0] is 0 and the last shard's value is 1536. `segment_ends`: a value of 512 means that the shard's first document runs to its end; shard 1 has the value 1 and the last shard the value 512.
All inputs are finite; a program needn't handle non-finite values.
Results may differ from the reference program's by a relative error of at most 0.012.
The reference program's roundings to bfloat16 on the way (of `shifted`, `probs_half` and `grad_scores`) count: a program that leaves them out, or rounds other values in their place, can miss the bound.
Values may be sent and summed in bfloat16 or wider, within the bound.
A program may use at most 128 MiB of HBM per device.

```python
import math
import jax
import jax.numpy as jnp
from jax import lax

HEADS = 40
HEAD = 128
WIDTH = 5120
TOK_CTX = 512
MEM = 1536
SHARDS = 64
TOKENS = 32768


def draw_queries(key, part):
    drawn = jax.random.truncated_normal(jax.random.fold_in(key, 21), -6.0, 6.0, (TOKENS, WIDTH), jnp.float32)
    result = drawn
    return result.astype(jnp.bfloat16)


def draw_keys(key, part):
    drawn = jax.random.truncated_normal(jax.random.fold_in(key, 22), -6.0, 6.0, (TOKENS, WIDTH), jnp.float32)
    result = drawn
    return result.astype(jnp.bfloat16)


def draw_memory_lengths(key, part):
    whole_memory = jax.random.randint(jax.random.fold_in(key, 31), (SHARDS,), 0, 2, dtype=jnp.int32)
    random_length = jax.random.randint(jax.random.fold_in(key, 32), (SHARDS,), 0, MEM + 1, dtype=jnp.int32)
    shard_index = jnp.arange(SHARDS, dtype=jnp.int32)
    picked = jnp.where(whole_memory == 1, MEM, random_length)
    picked = jnp.where(shard_index == 0, 0, picked)
    picked = jnp.where(shard_index == SHARDS - 1, MEM, picked)
    return picked.astype(jnp.int32)


def draw_segment_ends(key, part):
    whole_shard = jax.random.randint(jax.random.fold_in(key, 41), (SHARDS,), 0, 2, dtype=jnp.int32)
    random_end = jax.random.randint(jax.random.fold_in(key, 42), (SHARDS,), 1, TOK_CTX, dtype=jnp.int32)
    shard_index = jnp.arange(SHARDS, dtype=jnp.int32)
    picked = jnp.where(whole_shard == 1, TOK_CTX, random_end)
    picked = jnp.where(shard_index == 1, 1, picked)
    picked = jnp.where(shard_index == SHARDS - 1, TOK_CTX, picked)
    return picked.astype(jnp.int32)


def steps_of(stream_key, dims, split, smallest, top_value):
    def one(axis_at, blocks):
        steps = jax.random.uniform(jax.random.fold_in(jax.random.fold_in(stream_key, 6), axis_at), (blocks,), jnp.float32, smallest / len(split), top_value / len(split))
        return jnp.repeat(jnp.exp(steps), dims[axis_at] // blocks).reshape((-1,) + (1,) * (len(dims) - axis_at - 1))

    gain = one(*split[0])
    for cut in split[1:]:
        gain = gain * one(*cut)
    return gain


def scatter_about(own_key, shape, spread, most, split=(), kind=jnp.bfloat16):
    level = steps_of(own_key, shape, split, -0.22, 0.18) if split else 1.0
    entries = jax.random.normal(own_key, shape, jnp.float32) * spread * level
    return jnp.minimum(jnp.maximum(entries, -most), most).astype(kind)


def setup_inputs(seed: int = 0) -> dict:
    arg_keys = jax.random.split(jax.random.key(seed), 8)
    return {
        "queries": draw_queries(jax.random.fold_in(arg_keys[7], 71), 0),
        "keys": draw_keys(jax.random.fold_in(arg_keys[7], 71), 0),
        "values": scatter_about(arg_keys[2], (TOKENS, WIDTH), 1.0, 6.0, ((0, 256),)),
        "cotangent": scatter_about(arg_keys[3], (TOKENS, WIDTH), 1.0, 6.0, ((0, 256),)),
        "content_bias": scatter_about(arg_keys[4], (HEADS, HEAD), 1.0, 5.0, ((0, 4),), jnp.float32),
        "memory_lengths": draw_memory_lengths(jax.random.fold_in(arg_keys[7], 71), 0),
        "segment_ends": draw_segment_ends(jax.random.fold_in(arg_keys[7], 71), 0),
    }


def shard_pass(shard_index, queries, keys_padded, values_padded, cotangent, content_bias, memory_lengths, segment_ends):
    first_row = shard_index * TOK_CTX
    span_rows = MEM + TOK_CTX
    query_rows = lax.dynamic_slice_in_dim(queries, first_row, TOK_CTX, 0).astype(jnp.float32).reshape(TOK_CTX, HEADS, HEAD)
    key_rows = lax.dynamic_slice_in_dim(keys_padded, first_row, span_rows, 0).astype(jnp.float32).reshape(span_rows, HEADS, HEAD)
    value_rows = lax.dynamic_slice_in_dim(values_padded, first_row, span_rows, 0).astype(jnp.float32).reshape(span_rows, HEADS, HEAD)
    grad_rows = lax.dynamic_slice_in_dim(cotangent, first_row, TOK_CTX, 0).astype(jnp.float32).reshape(TOK_CTX, HEADS, HEAD)
    usable = jnp.minimum(memory_lengths[shard_index], first_row)
    boundary = segment_ends[shard_index]
    row_index = lax.broadcasted_iota(jnp.int32, (TOK_CTX, span_rows), 0)
    col_index = lax.broadcasted_iota(jnp.int32, (TOK_CTX, span_rows), 1)
    offset = col_index - MEM
    memory_ok = (col_index < MEM) & (col_index >= MEM - usable) & (row_index < boundary)
    local_ok = (col_index >= MEM) & (offset <= row_index) & ((row_index < boundary) == (offset < boundary))
    allowed = (memory_ok | local_ok)[None]
    scaling = 1.0 / math.sqrt(HEAD)
    shifted_half = (query_rows + content_bias[None]).astype(jnp.bfloat16)
    shifted = lax.optimization_barrier(shifted_half).astype(jnp.float32)
    highest = lax.Precision.HIGHEST
    scores = jnp.einsum('the,she->hts', shifted, key_rows, precision=highest) * scaling
    scores = jnp.where(allowed, scores, -jnp.inf)
    row_peak = lax.optimization_barrier(jnp.max(scores, axis=2, keepdims=True))
    weights = jnp.exp(scores - row_peak)
    probs_full = weights / lax.optimization_barrier(jnp.sum(weights, axis=2, keepdims=True))
    probs_half = lax.optimization_barrier(probs_full.astype(jnp.bfloat16)).astype(jnp.float32)
    attended = jnp.einsum('hts,she->the', probs_half, value_rows, precision=highest)
    grad_probs = jnp.einsum('the,she->hts', grad_rows, value_rows, precision=highest)
    centre = lax.optimization_barrier(jnp.sum(probs_full * grad_probs, axis=2, keepdims=True))
    grad_scores = lax.optimization_barrier((probs_full * (grad_probs - centre) * scaling).astype(jnp.bfloat16)).astype(jnp.float32)
    grad_query = jnp.einsum('hts,she->the', grad_scores, key_rows, precision=highest)
    grad_key = jnp.einsum('hts,the->she', grad_scores[:, :, MEM:], shifted, precision=highest)
    grad_value = jnp.einsum('hts,the->she', probs_half[:, :, MEM:], grad_rows, precision=highest)
    return (attended.reshape(TOK_CTX, WIDTH).astype(jnp.bfloat16), grad_query.reshape(TOK_CTX, WIDTH).astype(jnp.bfloat16), grad_key.reshape(TOK_CTX, WIDTH).astype(jnp.bfloat16), grad_value.reshape(TOK_CTX, WIDTH).astype(jnp.bfloat16), lax.optimization_barrier(jnp.sum(grad_query, axis=0)))

def reference(queries, keys, values, cotangent, content_bias, memory_lengths, segment_ends):
    padding = jnp.zeros((MEM, WIDTH), jnp.bfloat16)
    keys_padded = jnp.concatenate([padding, keys], axis=0)
    values_padded = jnp.concatenate([padding, values], axis=0)

    def one_shard(shard_index):
        return shard_pass(shard_index, queries, keys_padded, values_padded, cotangent, content_bias, memory_lengths, segment_ends)
    results = lax.map(one_shard, jnp.arange(SHARDS, dtype=jnp.int32))
    attended = results[0].reshape(TOKENS, WIDTH)
    grad_queries = results[1].reshape(TOKENS, WIDTH)
    grad_keys = results[2].reshape(TOKENS, WIDTH)
    grad_values = results[3].reshape(TOKENS, WIDTH)
    grad_bias = lax.optimization_barrier(jnp.sum(results[4], axis=0))
    return (attended, grad_queries, grad_keys, grad_values, grad_bias)
```

```python
import functools
import math

import jax
import jax.numpy as jnp
from jax import lax
from jax.experimental import pallas as pl
from jax.experimental.pallas import tpu as pltpu
from jax.sharding import PartitionSpec as P

MESH = pl.DeviceIdType.MESH
MEM = 1536
ROWS = 512
PART = 128
HEAD = 128
TSP = 4
RING = 4
LOCAL = 5
SPAN = MEM + 2 * ROWS
WIDE = MEM + ROWS
HALF = 256
MASKED = -1e30
SCALING = 1.0 / math.sqrt(HEAD)
LOG2_SCALING = SCALING * math.log2(math.e)
LAST = (((1,), (1,)), ((), ()))
FIRST = (((0,), (0,)), ((), ()))


def kernel(
    depth,
    q_ref, k_ref, v_ref, g_ref, bias_ref, length_ref, end_ref,
    o_ref, gq_ref, gk_ref, gv_ref, gb_ref,
    q_buf, g_buf, k_buf, v_buf, o_buf, gq_buf, gk_buf, gv_buf,
    info, mask, part_bias, z_bias, y_bias, sum_bias,
    in_send, in_recv, mem_send, mem_recv, out_send, out_recv, info_sem, z_sem, y_sem,
):
    c, t = lax.axis_index("ctx"), lax.axis_index("tsp")
    shards = depth * RING * 2
    core = lax.rem(c, 2)
    pair = c // 2
    y = lax.rem(pair, RING)
    z = pair // RING

    def far(value, n):
        return lax.rem(value, n)

    def x_peer(dk, dt):
        return (pair * 2 + (core if dk == 0 else 1 - core), far(t + dt, TSP))

    def z_peer(dz):
        return ((far(z + dz, depth) * RING + y) * 2 + core, t)

    def y_peer(dk, dy):
        return ((z * RING + far(y + dy, RING)) * 2 + (core if dk == 0 else 1 - core), t)

    def ctx_peer(step):
        return (far(c + step + shards, shards), t)

    x_peers = [(dk, dt) for dt in (1, 2, 3) for dk in (0, 1)] + [(1, 0)]
    y_peers = [(dk, dy) for dy in (1, 2, 3) for dk in (0, 1)] + [(1, 0)]

    barrier = pltpu.get_barrier_semaphore()

    def greet(device):
        pl.semaphore_signal(barrier, inc=1, device_id=device, device_id_type=MESH)

    for dk, dt in x_peers:
        greet(x_peer(dk, dt))
    for dz in range(1, depth):
        greet(z_peer(dz))
    for dk, dy in y_peers:
        greet(y_peer(dk, dy))
    greet(ctx_peer(-2))
    greet(ctx_peer(-4))
    pl.semaphore_wait(barrier, 7 + depth - 1 + 7 + 2)

    sources = (k_ref, v_ref, q_ref, g_ref)
    own_rows = pl.ds(pl.multiple_of(t * PART, PART), PART)

    def landing(which, head, shard, rows):
        if which < 2:
            first = MEM + shard * ROWS
            buf = (k_buf, v_buf)[which]
        else:
            first = shard * ROWS
            buf = (q_buf, g_buf)[which - 2]
        return buf.at[head, pl.ds(pl.multiple_of(first + rows, PART), PART)]

    def scatter_in(arrays, head):
        for dk, dt in x_peers + [(0, 0)]:
            device = x_peer(dk, dt)
            to_core = core if dk == 0 else 1 - core
            column = (device[1] * 2 + to_core) * LOCAL + head
            columns = pl.ds(pl.multiple_of(column * HEAD, HEAD), HEAD)
            for which in arrays:
                source = sources[which].at[:, columns]
                target = landing(which, head, core, t * PART)
                if (dk, dt) == (0, 0):
                    pltpu.make_async_copy(source, target, in_recv.at[which, head]).start()
                else:
                    pltpu.make_async_remote_copy(
                        source, target, in_send.at[which], in_recv.at[which, head],
                        device_id=device, device_id_type=MESH,
                    ).start()

    def wait_in(arrays, head):
        for which in arrays:
            if which < 2:
                ref = (k_buf, v_buf)[which].at[head, pl.ds(MEM, 2 * ROWS)]
            else:
                ref = (q_buf, g_buf)[which - 2].at[head]
            pltpu.make_async_copy(ref, ref, in_recv.at[which, head]).wait()

    def send_memory(head):
        for which, buf in enumerate((k_buf, v_buf)):
            pltpu.make_async_remote_copy(
                buf.at[head, pl.ds(MEM, 2 * ROWS)], buf.at[head, pl.ds(ROWS, 2 * ROWS)],
                mem_send.at[which], mem_recv.at[which, head],
                device_id=ctx_peer(2), device_id_type=MESH,
            ).start()
            pltpu.make_async_remote_copy(
                buf.at[head, pl.ds(MEM + ROWS, ROWS)], buf.at[head, pl.ds(0, ROWS)],
                mem_send.at[which], mem_recv.at[which, head],
                device_id=ctx_peer(4), device_id_type=MESH,
            ).start()

    def wait_memory(head):
        for which, buf in enumerate((k_buf, v_buf)):
            ref = buf.at[head, pl.ds(0, MEM)]
            pltpu.make_async_copy(ref, ref, mem_recv.at[which, head]).wait()

    def first_sends(head, carry):
        scatter_in((0, 1), head)
        return carry

    lax.fori_loop(0, 3, first_sends, 0)

    usable = jnp.minimum(length_ref[0], c * ROWS)
    tile_row = lax.broadcasted_iota(jnp.int32, (8, 128), 0)
    info[core] = jnp.where(tile_row == 0, usable, end_ref[0]).astype(jnp.float32)
    swap = pltpu.make_async_remote_copy(
        info.at[core], info.at[core], info_sem.at[0], info_sem.at[1],
        device_id=x_peer(1, 0), device_id_type=MESH,
    )
    swap.start()
    swap.wait()

    def build_mask(step, carry):
        shard, block = step // (WIDE // 128), lax.rem(step, WIDE // 128)
        limit = info[shard]
        allowed_memory = limit[0:1]
        boundary = limit[1:2]
        row = lax.broadcasted_iota(jnp.int32, (ROWS, 128), 0).astype(jnp.float32)
        col = (lax.broadcasted_iota(jnp.int32, (ROWS, 128), 1) + block * 128).astype(jnp.float32)
        offset = col - float(MEM)
        row_first = jnp.where(row < boundary, 1.0, 0.0)
        col_first = jnp.where(offset < boundary, 1.0, 0.0)
        memory_ok = jnp.where(offset >= 0.0 - allowed_memory, row_first, 0.0)
        local_ok = jnp.where((offset <= row) & (row_first == col_first), 1.0, 0.0)
        ok = jnp.where(offset < 0.0, memory_ok, local_ok)
        mask[shard, :, pl.ds(pl.multiple_of(block * 128, 128), 128)] = jnp.where(ok > 0.5, 0.0, MASKED)
        return carry

    lax.fori_loop(0, 2 * (WIDE // 128), build_mask, 0)

    def gather_step(head, carry):
        @pl.when(head < LOCAL - 3)
        def _():
            scatter_in((0, 1), head + 3)

        @pl.when(head >= LOCAL - 3)
        def _():
            scatter_in((2, 3), head - (LOCAL - 3))

        wait_in((0, 1), head)

        @pl.when(head < 2)
        def _():
            send_memory(head)

        return carry

    lax.fori_loop(0, LOCAL, gather_step, 0)

    def last_sends(head, carry):
        scatter_in((2, 3), head)
        return carry

    lax.fori_loop(3, LOCAL, last_sends, 0)

    outputs = ((o_buf, o_ref), (gq_buf, gq_ref), (gk_buf, gk_ref), (gv_buf, gv_ref))

    def attend(head, shard):
        bias = bias_ref[pl.ds(core * LOCAL + head, 1), :]
        key_first = pl.multiple_of(shard * ROWS, ROWS)
        bias_total = jnp.zeros((8, HEAD), jnp.float32)
        key_parts, value_parts = [], []
        for half in range(2):
            rows = pl.ds(half * HALF, HALF)
            in_rows = pl.ds(pl.multiple_of(shard * ROWS + half * HALF, HALF), HALF)
            span = MEM + HALF * (half + 1)
            shifted = (q_buf[head, in_rows, :].astype(jnp.float32) + bias).astype(jnp.bfloat16)
            grad_rows = g_buf[head, in_rows, :]
            key_rows = k_buf[head, pl.ds(key_first, span), :]
            value_rows = v_buf[head, pl.ds(key_first, span), :]
            scores = lax.dot_general(shifted, key_rows, LAST, preferred_element_type=jnp.float32)
            scores = scores * LOG2_SCALING + mask[shard, rows, 0:span]
            peak = jnp.max(scores, axis=1, keepdims=True)
            weights = jnp.exp2(scores - peak)
            inverse = 1.0 / jnp.sum(weights, axis=1, keepdims=True)
            probs = weights * inverse
            probs_half = probs.astype(jnp.bfloat16)
            attended = jnp.dot(probs_half, value_rows, preferred_element_type=jnp.float32)
            grad_probs = lax.dot_general(grad_rows, value_rows, LAST, preferred_element_type=jnp.float32)
            centre = jnp.sum(probs * grad_probs, axis=1, keepdims=True)
            grad_scores = (probs * (grad_probs - centre) * SCALING).astype(jnp.bfloat16)
            grad_query = jnp.dot(grad_scores, key_rows, preferred_element_type=jnp.float32)
            out_rows = in_rows
            o_buf[head, out_rows, :] = attended.astype(jnp.bfloat16)
            gq_buf[head, out_rows, :] = grad_query.astype(jnp.bfloat16)
            bias_total += jnp.sum(grad_query.reshape(HALF // 8, 8, HEAD), axis=0)
            key_parts.append(
                lax.dot_general(grad_scores[:, MEM:], shifted, FIRST, preferred_element_type=jnp.float32)
            )
            value_parts.append(
                lax.dot_general(probs_half[:, MEM:], grad_rows, FIRST, preferred_element_type=jnp.float32)
            )
        for buf, parts in ((gk_buf, key_parts), (gv_buf, value_parts)):
            low = pl.ds(pl.multiple_of(shard * ROWS, HALF), HALF)
            high = pl.ds(pl.multiple_of(shard * ROWS + HALF, HALF), HALF)
            buf[head, low, :] = (parts[0] + parts[1][:HALF]).astype(jnp.bfloat16)
            buf[head, high, :] = parts[1][HALF:].astype(jnp.bfloat16)
        return bias_total

    def send_out(head, shard, dt, local):
        to_part = far(t + dt, TSP)
        column = (t * 2 + core) * LOCAL + head
        columns = pl.ds(pl.multiple_of(column * HEAD, HEAD), HEAD)
        rows = pl.ds(pl.multiple_of(shard * ROWS + to_part * PART, PART), PART)
        for which, (buf, ref) in enumerate(outputs):
            source, target = buf.at[head, rows], ref.at[:, columns]
            if local:
                pltpu.make_async_copy(source, target, out_recv.at[which]).start()
            else:
                pltpu.make_async_remote_copy(
                    source, target, out_send.at[which], out_recv.at[which],
                    device_id=(pair * 2 + shard, to_part), device_id_type=MESH,
                ).start()

    def head_step(head, carry):
        wait_memory(head)

        @pl.when(head < LOCAL - 2)
        def _():
            send_memory(head + 2)

        wait_in((2, 3), head)

        def shard_step(i, total):
            shard = far(core + 1 + i, 2)
            total = total + attend(head, shard)
            for dt in (2, 1, 3):
                send_out(head, shard, dt, False)

            @pl.when(i == 0)
            def _():
                send_out(head, shard, 0, False)

            @pl.when(i == 1)
            def _():
                send_out(head, shard, 0, True)

            return total

        part_bias[head] = lax.fori_loop(0, 2, shard_step, jnp.zeros((8, HEAD), jnp.float32))
        return carry

    lax.fori_loop(0, LOCAL, head_step, 0)

    z_bias[z] = part_bias[...]
    for dz in range(1, depth):
        pltpu.make_async_remote_copy(
            part_bias, z_bias.at[z], z_sem.at[0], z_sem.at[1],
            device_id=z_peer(dz), device_id_type=MESH,
        ).start()
    others = z_bias.at[pl.ds(0, depth - 1)]
    pltpu.make_async_copy(others, others, z_sem.at[1]).wait()
    sum_bias[...] = jnp.sum(z_bias[...], axis=0)
    y_bias[core, y] = sum_bias[...]
    for dk, dy in y_peers:
        pltpu.make_async_remote_copy(
            sum_bias, y_bias.at[core, y], y_sem.at[0], y_sem.at[1],
            device_id=y_peer(dk, dy), device_id_type=MESH,
        ).start()
    others_y = z_bias.at[pl.ds(0, 7)]
    pltpu.make_async_copy(others_y, others_y, y_sem.at[1]).wait()
    for which in range(2):
        total = jnp.sum(jnp.sum(y_bias[which], axis=0), axis=1)
        gb_ref[pl.ds(which * LOCAL, LOCAL), :] = total

    for which in range(4):
        ref = outputs[which][1]
        pltpu.make_async_copy(ref, ref, out_recv.at[which]).wait()
        part = ref.at[:, pl.ds(0, 7 * LOCAL * HEAD)]
        pltpu.make_async_copy(part, part, out_send.at[which]).wait()
        pltpu.make_async_copy(part, part, in_send.at[which]).wait()
    for which, buf in enumerate((k_buf, v_buf)):
        ref = buf.at[:, pl.ds(0, MEM)]
        pltpu.make_async_copy(ref, ref, mem_send.at[which]).wait()
    pltpu.make_async_copy(others, others, z_sem.at[0]).wait()
    pltpu.make_async_copy(others_y, others_y, y_sem.at[0]).wait()


def solution(mesh):
    depth = mesh.shape["ctx"] // (2 * RING)
    half = jnp.bfloat16

    def step(queries, keys, values, cotangent, content_bias, memory_lengths, segment_ends):
        any_spec = pl.BlockSpec(memory_space=pl.ANY)
        vmem_spec = pl.BlockSpec(memory_space=pltpu.VMEM)
        smem_spec = pl.BlockSpec(memory_space=pltpu.SMEM)
        slab = jax.ShapeDtypeStruct(queries.shape, half)
        dma, vmem = pltpu.SemaphoreType.DMA, pltpu.VMEM
        return pl.pallas_call(
            functools.partial(kernel, depth),
            out_shape=(slab, slab, slab, slab, jax.ShapeDtypeStruct(content_bias.shape, jnp.float32)),
            in_specs=[any_spec] * 4 + [vmem_spec, smem_spec, smem_spec],
            out_specs=[any_spec] * 4 + [vmem_spec],
            scratch_shapes=[
                vmem((LOCAL, 2 * ROWS, HEAD), half),
                vmem((LOCAL, 2 * ROWS, HEAD), half),
                vmem((LOCAL, SPAN, HEAD), half),
                vmem((LOCAL, SPAN, HEAD), half),
                vmem((LOCAL, 2 * ROWS, HEAD), half),
                vmem((LOCAL, 2 * ROWS, HEAD), half),
                vmem((LOCAL, 2 * ROWS, HEAD), half),
                vmem((LOCAL, 2 * ROWS, HEAD), half),
                vmem((2, 8, 128), jnp.float32),
                vmem((2, ROWS, WIDE), jnp.float32),
                vmem((LOCAL, 8, HEAD), jnp.float32),
                vmem((depth, LOCAL, 8, HEAD), jnp.float32),
                vmem((2, RING, LOCAL, 8, HEAD), jnp.float32),
                vmem((LOCAL, 8, HEAD), jnp.float32),
                dma((4,)),
                dma((4, LOCAL)),
                dma((2,)),
                dma((2, LOCAL)),
                dma((4,)),
                dma((4,)),
                dma((2,)),
                dma((2,)),
                dma((2,)),
            ],
            compiler_params=pltpu.CompilerParams(
                collective_id=1, has_side_effects=True, vmem_limit_bytes=60 * 1024 * 1024
            ),
            cost_estimate=pl.CostEstimate(flops=12 * 10**9, bytes_accessed=20 * 10**6, transcendentals=10**7),
        )(queries, keys, values, cotangent, content_bias, memory_lengths, segment_ends)

    tokens = P(("ctx", "tsp"), None)
    return jax.shard_map(
        step,
        mesh=mesh,
        in_specs=(tokens, tokens, tokens, tokens, P("tsp", None), P("ctx"), P("ctx")),
        out_specs=(tokens, tokens, tokens, tokens, P("tsp", None)),
        check_vma=False,
    )
```

```python
import functools
import math

import jax
import jax.numpy as jnp
from jax import lax
from jax.experimental import pallas as pl
from jax.experimental.pallas import tpu as pltpu
from jax.sharding import PartitionSpec as P

MESH = pl.DeviceIdType.MESH
MEM = 1536
ROWS = 512
PART = 128
HEAD = 128
TSP = 4
RING = 4
LOCAL = 5
SPAN = MEM + 2 * ROWS
WIDE = MEM + ROWS
HALF = 256
AHEAD = 2
VLIMIT = 48
MASKED = -1e30
SCALING = 1.0 / math.sqrt(HEAD)
LOG2_SCALING = SCALING * math.log2(math.e)
LAST = (((1,), (1,)), ((), ()))
FIRST = (((0,), (0,)), ((), ()))


def kernel(
    depth,
    q_ref, k_ref, v_ref, g_ref, bias_ref, length_ref, end_ref,
    o_ref, gq_ref, gk_ref, gv_ref, gb_ref,
    q_buf, g_buf, k_buf, v_buf, o_buf, gq_buf, gk_buf, gv_buf,
    k_relay, v_relay, info, mask, part_bias, z_bias, y_bias, sum_bias,
    in_send, in_recv, mem_send, mem_recv, relay_send, relay_recv, out_send, out_recv, info_sem, z_sem, y_sem,
):
    c, t = lax.axis_index("ctx"), lax.axis_index("tsp")
    shards = depth * RING * 2
    core = lax.rem(c, 2)
    pair = c // 2
    y = lax.rem(pair, RING)
    z = pair // RING

    def far(value, n):
        return lax.rem(value, n)

    def x_peer(dk, dt):
        return (pair * 2 + (core if dk == 0 else 1 - core), far(t + dt, TSP))

    def z_peer(dz):
        return ((far(z + dz, depth) * RING + y) * 2 + core, t)

    def y_peer(dk, dy):
        return ((z * RING + far(y + dy, RING)) * 2 + (core if dk == 0 else 1 - core), t)

    def ctx_peer(step):
        return (far(c + step + shards, shards), t)

    def place(z_at, y_at):
        return ((far(z_at + depth, depth) * RING + far(y_at + RING, RING)) * 2 + core, t)

    relay_to = place(z, y - 1)
    relay_from = place(z, y + 1)
    onward_to = place(z + jnp.where((y == 1) | (y == 2), 1, 0), y - 1)
    onward_from = place(z - jnp.where((y == 0) | (y == 1), 1, 0), y + 1)

    x_peers = [(dk, dt) for dt in (1, 2, 3) for dk in (0, 1)] + [(1, 0)]
    y_peers = [(dk, dy) for dy in (1, 2, 3) for dk in (0, 1)] + [(1, 0)]

    barrier = pltpu.get_barrier_semaphore()

    def greet(device):
        pl.semaphore_signal(barrier, inc=1, device_id=device, device_id_type=MESH)

    for dk, dt in x_peers:
        greet(x_peer(dk, dt))
    for dz in range(1, depth):
        greet(z_peer(dz))
    for dk, dy in y_peers:
        greet(y_peer(dk, dy))
    greet(ctx_peer(-2))
    greet(relay_from)
    greet(onward_from)
    pl.semaphore_wait(barrier, 7 + depth - 1 + 7 + 3)

    sources = (k_ref, v_ref, q_ref, g_ref)
    own_rows = pl.ds(pl.multiple_of(t * PART, PART), PART)

    def landing(which, head, shard, rows):
        if which < 2:
            first = MEM + shard * ROWS
            buf = (k_buf, v_buf)[which]
        else:
            first = shard * ROWS
            buf = (q_buf, g_buf)[which - 2]
        return buf.at[head, pl.ds(pl.multiple_of(first + rows, PART), PART)]

    def scatter_in(arrays, head):
        for dk, dt in x_peers + [(0, 0)]:
            device = x_peer(dk, dt)
            to_core = core if dk == 0 else 1 - core
            column = (device[1] * 2 + to_core) * LOCAL + head
            columns = pl.ds(pl.multiple_of(column * HEAD, HEAD), HEAD)
            for which in arrays:
                source = sources[which].at[:, columns]
                target = landing(which, head, core, t * PART)
                if (dk, dt) == (0, 0):
                    pltpu.make_async_copy(source, target, in_recv.at[which, head]).start()
                else:
                    pltpu.make_async_remote_copy(
                        source, target, in_send.at[which], in_recv.at[which, head],
                        device_id=device, device_id_type=MESH,
                    ).start()

    def wait_in(arrays, head):
        for which in arrays:
            if which < 2:
                ref = (k_buf, v_buf)[which].at[head, pl.ds(MEM, 2 * ROWS)]
            else:
                ref = (q_buf, g_buf)[which - 2].at[head]
            pltpu.make_async_copy(ref, ref, in_recv.at[which, head]).wait()

    def send_memory(head):
        for which, buf in enumerate((k_buf, v_buf)):
            pltpu.make_async_remote_copy(
                buf.at[head, pl.ds(MEM, 2 * ROWS)], buf.at[head, pl.ds(ROWS, 2 * ROWS)],
                mem_send.at[which], mem_recv.at[which, head],
                device_id=ctx_peer(2), device_id_type=MESH,
            ).start()
            pltpu.make_async_remote_copy(
                buf.at[head, pl.ds(MEM + ROWS, ROWS)], (k_relay, v_relay)[which].at[head],
                relay_send.at[which], relay_recv.at[which, head],
                device_id=relay_to, device_id_type=MESH,
            ).start()

    def forward(head):
        for which, (relay, buf) in enumerate(((k_relay, k_buf), (v_relay, v_buf))):
            pltpu.make_async_copy(relay.at[head], relay.at[head], relay_recv.at[which, head]).wait()
            pltpu.make_async_remote_copy(
                relay.at[head], buf.at[head, pl.ds(0, ROWS)],
                mem_send.at[which], mem_recv.at[which, head],
                device_id=onward_to, device_id_type=MESH,
            ).start()

    def wait_memory(head):
        for which, buf in enumerate((k_buf, v_buf)):
            ref = buf.at[head, pl.ds(0, MEM)]
            pltpu.make_async_copy(ref, ref, mem_recv.at[which, head]).wait()

    def first_sends(head, carry):
        scatter_in((0, 1), head)
        return carry

    lax.fori_loop(0, AHEAD, first_sends, 0)

    usable = jnp.minimum(length_ref[0], c * ROWS)
    tile_row = lax.broadcasted_iota(jnp.int32, (8, 128), 0)
    info[core] = jnp.where(tile_row == 0, usable, end_ref[0]).astype(jnp.float32)
    swap = pltpu.make_async_remote_copy(
        info.at[core], info.at[core], info_sem.at[0], info_sem.at[1],
        device_id=x_peer(1, 0), device_id_type=MESH,
    )
    swap.start()
    swap.wait()

    def build_mask(step, carry):
        shard, block = step // (WIDE // 128), lax.rem(step, WIDE // 128)
        limit = info[shard]
        allowed_memory = limit[0:1]
        boundary = limit[1:2]
        row = lax.broadcasted_iota(jnp.int32, (ROWS, 128), 0).astype(jnp.float32)
        col = (lax.broadcasted_iota(jnp.int32, (ROWS, 128), 1) + block * 128).astype(jnp.float32)
        offset = col - float(MEM)
        row_first = jnp.where(row < boundary, 1.0, 0.0)
        col_first = jnp.where(offset < boundary, 1.0, 0.0)
        memory_ok = jnp.where(offset >= 0.0 - allowed_memory, row_first, 0.0)
        local_ok = jnp.where((offset <= row) & (row_first == col_first), 1.0, 0.0)
        ok = jnp.where(offset < 0.0, memory_ok, local_ok)
        mask[shard, :, pl.ds(pl.multiple_of(block * 128, 128), 128)] = jnp.where(ok > 0.5, 0.0, MASKED)
        return carry

    lax.fori_loop(0, 2 * (WIDE // 128), build_mask, 0)

    def gather_step(head, carry):
        wait_in((0, 1), head)

        @pl.when(head < 2)
        def _():
            send_memory(head)

        @pl.when(head < LOCAL - AHEAD)
        def _():
            scatter_in((0, 1), head + AHEAD)

        @pl.when(head >= LOCAL - AHEAD)
        def _():
            scatter_in((2, 3), head - (LOCAL - AHEAD))

        @pl.when((head >= 2) & (head < 4))
        def _():
            forward(head - 2)

        return carry

    lax.fori_loop(0, LOCAL, gather_step, 0)

    def last_sends(head, carry):
        scatter_in((2, 3), head)
        return carry

    lax.fori_loop(AHEAD, LOCAL, last_sends, 0)

    outputs = ((o_buf, o_ref), (gq_buf, gq_ref), (gk_buf, gk_ref), (gv_buf, gv_ref))

    def attend(head, shard):
        bias = bias_ref[pl.ds(core * LOCAL + head, 1), :]
        key_first = pl.multiple_of(shard * ROWS, ROWS)
        bias_total = jnp.zeros((8, HEAD), jnp.float32)
        key_parts, value_parts = [], []
        for half in range(2):
            rows = pl.ds(half * HALF, HALF)
            in_rows = pl.ds(pl.multiple_of(shard * ROWS + half * HALF, HALF), HALF)
            span = MEM + HALF * (half + 1)
            shifted = (q_buf[head, in_rows, :].astype(jnp.float32) + bias).astype(jnp.bfloat16)
            grad_rows = g_buf[head, in_rows, :]
            key_rows = k_buf[head, pl.ds(key_first, span), :]
            value_rows = v_buf[head, pl.ds(key_first, span), :]
            scores = lax.dot_general(shifted, key_rows, LAST, preferred_element_type=jnp.float32)
            scores = scores * LOG2_SCALING + mask[shard, rows, 0:span]
            peak = jnp.max(scores, axis=1, keepdims=True)
            weights = jnp.exp2(scores - peak)
            inverse = 1.0 / jnp.sum(weights, axis=1, keepdims=True)
            probs = weights * inverse
            probs_half = probs.astype(jnp.bfloat16)
            attended = jnp.dot(probs_half, value_rows, preferred_element_type=jnp.float32)
            grad_probs = lax.dot_general(grad_rows, value_rows, LAST, preferred_element_type=jnp.float32)
            centre = jnp.sum(probs * grad_probs, axis=1, keepdims=True)
            grad_scores = (probs * (grad_probs - centre) * SCALING).astype(jnp.bfloat16)
            grad_query = jnp.dot(grad_scores, key_rows, preferred_element_type=jnp.float32)
            out_rows = in_rows
            o_buf[head, out_rows, :] = attended.astype(jnp.bfloat16)
            gq_buf[head, out_rows, :] = grad_query.astype(jnp.bfloat16)
            bias_total += jnp.sum(grad_query.reshape(HALF // 8, 8, HEAD), axis=0)
            key_parts.append(
                lax.dot_general(grad_scores[:, MEM:], shifted, FIRST, preferred_element_type=jnp.float32)
            )
            value_parts.append(
                lax.dot_general(probs_half[:, MEM:], grad_rows, FIRST, preferred_element_type=jnp.float32)
            )
        for buf, parts in ((gk_buf, key_parts), (gv_buf, value_parts)):
            low = pl.ds(pl.multiple_of(shard * ROWS, HALF), HALF)
            high = pl.ds(pl.multiple_of(shard * ROWS + HALF, HALF), HALF)
            buf[head, low, :] = (parts[0] + parts[1][:HALF]).astype(jnp.bfloat16)
            buf[head, high, :] = parts[1][HALF:].astype(jnp.bfloat16)
        return bias_total

    def send_out(head, shard, dt, local):
        to_part = far(t + dt, TSP)
        column = (t * 2 + core) * LOCAL + head
        columns = pl.ds(pl.multiple_of(column * HEAD, HEAD), HEAD)
        rows = pl.ds(pl.multiple_of(shard * ROWS + to_part * PART, PART), PART)
        for which, (buf, ref) in enumerate(outputs):
            source, target = buf.at[head, rows], ref.at[:, columns]
            if local:
                pltpu.make_async_copy(source, target, out_recv.at[which]).start()
            else:
                pltpu.make_async_remote_copy(
                    source, target, out_send.at[which], out_recv.at[which],
                    device_id=(pair * 2 + shard, to_part), device_id_type=MESH,
                ).start()

    def head_step(head, carry):
        wait_memory(head)

        @pl.when(head < LOCAL - 2)
        def _():
            send_memory(head + 2)

        wait_in((2, 3), head)

        def shard_step(i, total):
            shard = far(core + 1 + i, 2)
            total = total + attend(head, shard)
            for dt in (2, 1, 3):
                send_out(head, shard, dt, False)

            @pl.when(i == 0)
            def _():
                send_out(head, shard, 0, False)

            @pl.when(i == 1)
            def _():
                send_out(head, shard, 0, True)

            return total

        part_bias[head] = lax.fori_loop(0, 2, shard_step, jnp.zeros((8, HEAD), jnp.float32))

        @pl.when(head < LOCAL - 2)
        def _():
            forward(head + 2)

        return carry

    lax.fori_loop(0, LOCAL, head_step, 0)

    z_bias[z] = part_bias[...]
    for dz in range(1, depth):
        pltpu.make_async_remote_copy(
            part_bias, z_bias.at[z], z_sem.at[0], z_sem.at[1],
            device_id=z_peer(dz), device_id_type=MESH,
        ).start()
    others = z_bias.at[pl.ds(0, depth - 1)]
    pltpu.make_async_copy(others, others, z_sem.at[1]).wait()
    sum_bias[...] = jnp.sum(z_bias[...], axis=0)
    y_bias[core, y] = sum_bias[...]
    for dk, dy in y_peers:
        pltpu.make_async_remote_copy(
            sum_bias, y_bias.at[core, y], y_sem.at[0], y_sem.at[1],
            device_id=y_peer(dk, dy), device_id_type=MESH,
        ).start()
    others_y = z_bias.at[pl.ds(0, 7)]
    pltpu.make_async_copy(others_y, others_y, y_sem.at[1]).wait()
    for which in range(2):
        total = jnp.sum(jnp.sum(y_bias[which], axis=0), axis=1)
        gb_ref[pl.ds(which * LOCAL, LOCAL), :] = total

    for which in range(4):
        ref = outputs[which][1]
        pltpu.make_async_copy(ref, ref, out_recv.at[which]).wait()
        part = ref.at[:, pl.ds(0, 7 * LOCAL * HEAD)]
        pltpu.make_async_copy(part, part, out_send.at[which]).wait()
        pltpu.make_async_copy(part, part, in_send.at[which]).wait()
    for which, buf in enumerate((k_buf, v_buf)):
        ref = buf.at[:, pl.ds(0, MEM)]
        pltpu.make_async_copy(ref, ref, mem_send.at[which]).wait()
        relay = (k_relay, v_relay)[which]
        pltpu.make_async_copy(relay, relay, relay_send.at[which]).wait()
    pltpu.make_async_copy(others, others, z_sem.at[0]).wait()
    pltpu.make_async_copy(others_y, others_y, y_sem.at[0]).wait()


def write_out(o_in, gq_in, gk_in, gv_in, gb_in, o_ref, gq_ref, gk_ref, gv_ref, gb_ref, sem):
    pairs = ((o_in, o_ref), (gq_in, gq_ref), (gk_in, gk_ref), (gv_in, gv_ref), (gb_in, gb_ref))
    copies = [pltpu.make_async_copy(source, target, sem.at[i]) for i, (source, target) in enumerate(pairs)]
    for copy in copies:
        copy.start()
    for copy in copies:
        copy.wait()


def solution(mesh):
    depth = mesh.shape["ctx"] // (2 * RING)
    half = jnp.bfloat16

    def step(queries, keys, values, cotangent, content_bias, memory_lengths, segment_ends):
        any_spec = pl.BlockSpec(memory_space=pl.ANY)
        vmem_spec = pl.BlockSpec(memory_space=pltpu.VMEM)
        smem_spec = pl.BlockSpec(memory_space=pltpu.SMEM)
        slab = jax.ShapeDtypeStruct(queries.shape, half)
        dma, vmem = pltpu.SemaphoreType.DMA, pltpu.VMEM
        found = pl.pallas_call(
            functools.partial(kernel, depth),
            out_shape=(slab, slab, slab, slab, jax.ShapeDtypeStruct(content_bias.shape, jnp.float32)),
            in_specs=[any_spec] * 4 + [vmem_spec, smem_spec, smem_spec],
            out_specs=[any_spec] * 4 + [vmem_spec],
            scratch_shapes=[
                vmem((LOCAL, 2 * ROWS, HEAD), half),
                vmem((LOCAL, 2 * ROWS, HEAD), half),
                vmem((LOCAL, SPAN, HEAD), half),
                vmem((LOCAL, SPAN, HEAD), half),
                vmem((LOCAL, 2 * ROWS, HEAD), half),
                vmem((LOCAL, 2 * ROWS, HEAD), half),
                vmem((LOCAL, 2 * ROWS, HEAD), half),
                vmem((LOCAL, 2 * ROWS, HEAD), half),
                vmem((LOCAL, ROWS, HEAD), half),
                vmem((LOCAL, ROWS, HEAD), half),
                vmem((2, 8, 128), jnp.float32),
                vmem((2, ROWS, WIDE), jnp.float32),
                vmem((LOCAL, 8, HEAD), jnp.float32),
                vmem((depth, LOCAL, 8, HEAD), jnp.float32),
                vmem((2, RING, LOCAL, 8, HEAD), jnp.float32),
                vmem((LOCAL, 8, HEAD), jnp.float32),
                dma((4,)),
                dma((4, LOCAL)),
                dma((2,)),
                dma((2, LOCAL)),
                dma((2,)),
                dma((2, LOCAL)),
                dma((4,)),
                dma((4,)),
                dma((2,)),
                dma((2,)),
                dma((2,)),
            ],
            compiler_params=pltpu.CompilerParams(
                collective_id=1, has_side_effects=True, vmem_limit_bytes=VLIMIT * 1024 * 1024
            ),
            cost_estimate=pl.CostEstimate(flops=12 * 10**9, bytes_accessed=20 * 10**6, transcendentals=10**7),
        )(queries, keys, values, cotangent, content_bias, memory_lengths, segment_ends)
        return pl.pallas_call(
            write_out,
            out_shape=(slab, slab, slab, slab, jax.ShapeDtypeStruct(content_bias.shape, jnp.float32)),
            in_specs=[any_spec] * 5,
            out_specs=[any_spec] * 5,
            scratch_shapes=[dma((5,))],
            compiler_params=pltpu.CompilerParams(vmem_limit_bytes=16 * 1024 * 1024),
        )(*found)

    tokens = P(("ctx", "tsp"), None)
    return jax.shard_map(
        step,
        mesh=mesh,
        in_specs=(tokens, tokens, tokens, tokens, P("tsp", None), P("ctx"), P("ctx")),
        out_specs=(tokens, tokens, tokens, tokens, P("tsp", None)),
        check_vma=False,
    )
```

```python
import functools
import math

import jax
import jax.numpy as jnp
from jax import lax
from jax.experimental import pallas as pl
from jax.experimental.pallas import tpu as pltpu
from jax.sharding import PartitionSpec as P

MESH = pl.DeviceIdType.MESH
MEM = 1536
ROWS = 512
PART = 128
HEAD = 128
TSP = 4
RING = 4
LOCAL = 5
SPAN = MEM + 2 * ROWS
WIDE = MEM + ROWS
HALF = 256
AHEAD = 2
VLIMIT = 48
MASKED = -1e30
SCALING = 1.0 / math.sqrt(HEAD)
LOG2_SCALING = SCALING * math.log2(math.e)
LAST = (((1,), (1,)), ((), ()))
FIRST = (((0,), (0,)), ((), ()))


def kernel(
    depth,
    q_ref, k_ref, v_ref, g_ref, bias_ref, length_ref, end_ref,
    o_ref, gq_ref, gk_ref, gv_ref, gb_ref,
    q_buf, g_buf, k_buf, v_buf, o_buf, gq_buf, gk_buf, gv_buf,
    k_relay, v_relay, info, mask, part_bias, z_bias, y_bias, sum_bias,
    in_send, in_recv, mem_send, mem_recv, relay_send, relay_recv, out_send, out_recv, info_sem, z_sem, z_recv, y_sem, y_recv, hello,
):
    c, t = lax.axis_index("ctx"), lax.axis_index("tsp")
    shards = depth * RING * 2
    core = lax.rem(c, 2)
    pair = c // 2
    y = lax.rem(pair, RING)
    z = pair // RING

    def far(value, n):
        return lax.rem(value, n)

    def x_peer(dk, dt):
        return (pair * 2 + (core if dk == 0 else 1 - core), far(t + dt, TSP))

    def ctx_peer(step):
        return (far(c + step + shards, shards), t)

    def place(z_at, y_at):
        return ((far(z_at + depth, depth) * RING + far(y_at + RING, RING)) * 2 + core, t)

    relay_to = place(z, y - 1)
    relay_from = place(z, y + 1)
    onward_to = place(z + jnp.where((y == 1) | (y == 2), 1, 0), y - 1)
    onward_from = place(z - jnp.where((y == 0) | (y == 1), 1, 0), y + 1)

    x_peers = [(dk, dt) for dt in (1, 2, 3) for dk in (0, 1)] + [(1, 0)]

    barrier = pltpu.get_barrier_semaphore()

    def greet(device):
        pl.semaphore_signal(barrier, inc=1, device_id=device, device_id_type=MESH)

    for dk, dt in x_peers:
        greet(x_peer(dk, dt))
    greet(ctx_peer(-2))
    greet(relay_from)
    greet(onward_from)
    greet(place(z - 1, y))
    pl.semaphore_wait(barrier, 7 + 4)
    pl.semaphore_signal(hello, inc=1, device_id=place(z + 1, y), device_id_type=MESH)

    sources = (k_ref, v_ref, q_ref, g_ref)
    own_rows = pl.ds(pl.multiple_of(t * PART, PART), PART)

    def landing(which, head, shard, rows):
        if which < 2:
            first = MEM + shard * ROWS
            buf = (k_buf, v_buf)[which]
        else:
            first = shard * ROWS
            buf = (q_buf, g_buf)[which - 2]
        return buf.at[head, pl.ds(pl.multiple_of(first + rows, PART), PART)]

    def scatter_in(arrays, head):
        for dk, dt in x_peers + [(0, 0)]:
            device = x_peer(dk, dt)
            to_core = core if dk == 0 else 1 - core
            column = (device[1] * 2 + to_core) * LOCAL + head
            columns = pl.ds(pl.multiple_of(column * HEAD, HEAD), HEAD)
            for which in arrays:
                source = sources[which].at[:, columns]
                target = landing(which, head, core, t * PART)
                if (dk, dt) == (0, 0):
                    pltpu.make_async_copy(source, target, in_recv.at[which, head]).start()
                else:
                    pltpu.make_async_remote_copy(
                        source, target, in_send.at[which], in_recv.at[which, head],
                        device_id=device, device_id_type=MESH,
                    ).start()

    def wait_in(arrays, head):
        for which in arrays:
            if which < 2:
                ref = (k_buf, v_buf)[which].at[head, pl.ds(MEM, 2 * ROWS)]
            else:
                ref = (q_buf, g_buf)[which - 2].at[head]
            pltpu.make_async_copy(ref, ref, in_recv.at[which, head]).wait()

    def send_memory(head):
        for which, buf in enumerate((k_buf, v_buf)):
            pltpu.make_async_remote_copy(
                buf.at[head, pl.ds(MEM, 2 * ROWS)], buf.at[head, pl.ds(ROWS, 2 * ROWS)],
                mem_send.at[which], mem_recv.at[which, head],
                device_id=ctx_peer(2), device_id_type=MESH,
            ).start()
            pltpu.make_async_remote_copy(
                buf.at[head, pl.ds(MEM + ROWS, ROWS)], (k_relay, v_relay)[which].at[head],
                relay_send.at[which], relay_recv.at[which, head],
                device_id=relay_to, device_id_type=MESH,
            ).start()

    def forward(head):
        for which, (relay, buf) in enumerate(((k_relay, k_buf), (v_relay, v_buf))):
            pltpu.make_async_copy(relay.at[head], relay.at[head], relay_recv.at[which, head]).wait()
            pltpu.make_async_remote_copy(
                relay.at[head], buf.at[head, pl.ds(0, ROWS)],
                mem_send.at[which], mem_recv.at[which, head],
                device_id=onward_to, device_id_type=MESH,
            ).start()

    def wait_memory(head):
        for which, buf in enumerate((k_buf, v_buf)):
            ref = buf.at[head, pl.ds(0, MEM)]
            pltpu.make_async_copy(ref, ref, mem_recv.at[which, head]).wait()

    part_bias[...] = jnp.zeros_like(part_bias)

    def first_sends(head, carry):
        scatter_in((0, 1), head)
        return carry

    lax.fori_loop(0, AHEAD, first_sends, 0)

    usable = jnp.minimum(length_ref[0], c * ROWS)
    tile_row = lax.broadcasted_iota(jnp.int32, (8, 128), 0)
    info[core] = jnp.where(tile_row == 0, usable, end_ref[0]).astype(jnp.float32)
    swap = pltpu.make_async_remote_copy(
        info.at[core], info.at[core], info_sem.at[0], info_sem.at[1],
        device_id=x_peer(1, 0), device_id_type=MESH,
    )
    swap.start()
    swap.wait()

    def build_mask(step, carry):
        shard, block = step // (WIDE // 128), lax.rem(step, WIDE // 128)
        limit = info[shard]
        allowed_memory = limit[0:1]
        boundary = limit[1:2]
        row = lax.broadcasted_iota(jnp.int32, (ROWS, 128), 0).astype(jnp.float32)
        col = (lax.broadcasted_iota(jnp.int32, (ROWS, 128), 1) + block * 128).astype(jnp.float32)
        offset = col - float(MEM)
        row_first = jnp.where(row < boundary, 1.0, 0.0)
        col_first = jnp.where(offset < boundary, 1.0, 0.0)
        memory_ok = jnp.where(offset >= 0.0 - allowed_memory, row_first, 0.0)
        local_ok = jnp.where((offset <= row) & (row_first == col_first), 1.0, 0.0)
        ok = jnp.where(offset < 0.0, memory_ok, local_ok)
        mask[shard, :, pl.ds(pl.multiple_of(block * 128, 128), 128)] = jnp.where(ok > 0.5, 0.0, MASKED)
        return carry

    lax.fori_loop(0, 2 * (WIDE // 128), build_mask, 0)

    def gather_step(head, carry):
        wait_in((0, 1), head)

        @pl.when(head < 2)
        def _():
            send_memory(head)

        @pl.when(head < LOCAL - AHEAD)
        def _():
            scatter_in((0, 1), head + AHEAD)

        @pl.when(head >= LOCAL - AHEAD)
        def _():
            scatter_in((2, 3), head - (LOCAL - AHEAD))

        @pl.when((head >= 2) & (head < 4))
        def _():
            forward(head - 2)

        return carry

    lax.fori_loop(0, LOCAL, gather_step, 0)

    def last_sends(head, carry):
        scatter_in((2, 3), head)
        return carry

    lax.fori_loop(AHEAD, LOCAL, last_sends, 0)

    outputs = ((o_buf, o_ref), (gq_buf, gq_ref), (gk_buf, gk_ref), (gv_buf, gv_ref))

    def attend(head, shard):
        bias = bias_ref[pl.ds(core * LOCAL + head, 1), :]
        key_first = pl.multiple_of(shard * ROWS, ROWS)
        bias_total = jnp.zeros((8, HEAD), jnp.float32)
        key_parts, value_parts = [], []
        for half in range(2):
            rows = pl.ds(half * HALF, HALF)
            in_rows = pl.ds(pl.multiple_of(shard * ROWS + half * HALF, HALF), HALF)
            span = MEM + HALF * (half + 1)
            shifted = (q_buf[head, in_rows, :].astype(jnp.float32) + bias).astype(jnp.bfloat16)
            grad_rows = g_buf[head, in_rows, :]
            key_rows = k_buf[head, pl.ds(key_first, span), :]
            value_rows = v_buf[head, pl.ds(key_first, span), :]
            scores = lax.dot_general(shifted, key_rows, LAST, preferred_element_type=jnp.float32)
            scores = scores * LOG2_SCALING + mask[shard, rows, 0:span]
            peak = jnp.max(scores, axis=1, keepdims=True)
            weights = jnp.exp2(scores - peak)
            inverse = 1.0 / jnp.sum(weights, axis=1, keepdims=True)
            probs = weights * inverse
            probs_half = probs.astype(jnp.bfloat16)
            attended = jnp.dot(probs_half, value_rows, preferred_element_type=jnp.float32)
            grad_probs = lax.dot_general(grad_rows, value_rows, LAST, preferred_element_type=jnp.float32)
            centre = jnp.sum(probs * grad_probs, axis=1, keepdims=True)
            grad_scores = (probs * (grad_probs - centre) * SCALING).astype(jnp.bfloat16)
            grad_query = jnp.dot(grad_scores, key_rows, preferred_element_type=jnp.float32)
            out_rows = in_rows
            o_buf[head, out_rows, :] = attended.astype(jnp.bfloat16)
            gq_buf[head, out_rows, :] = grad_query.astype(jnp.bfloat16)
            bias_total += jnp.sum(grad_query.reshape(HALF // 8, 8, HEAD), axis=0)
            key_parts.append(
                lax.dot_general(grad_scores[:, MEM:], shifted, FIRST, preferred_element_type=jnp.float32)
            )
            value_parts.append(
                lax.dot_general(probs_half[:, MEM:], grad_rows, FIRST, preferred_element_type=jnp.float32)
            )
        for buf, parts in ((gk_buf, key_parts), (gv_buf, value_parts)):
            low = pl.ds(pl.multiple_of(shard * ROWS, HALF), HALF)
            high = pl.ds(pl.multiple_of(shard * ROWS + HALF, HALF), HALF)
            buf[head, low, :] = (parts[0] + parts[1][:HALF]).astype(jnp.bfloat16)
            buf[head, high, :] = parts[1][HALF:].astype(jnp.bfloat16)
        return bias_total

    def send_out(head, shard, dt, local):
        to_part = far(t + dt, TSP)
        column = (t * 2 + core) * LOCAL + head
        columns = pl.ds(pl.multiple_of(column * HEAD, HEAD), HEAD)
        rows = pl.ds(pl.multiple_of(shard * ROWS + to_part * PART, PART), PART)
        for which, (buf, ref) in enumerate(outputs):
            source, target = buf.at[head, rows], ref.at[:, columns]
            if local:
                pltpu.make_async_copy(source, target, out_recv.at[which]).start()
            else:
                pltpu.make_async_remote_copy(
                    source, target, out_send.at[which], out_recv.at[which],
                    device_id=(pair * 2 + shard, to_part), device_id_type=MESH,
                ).start()

    def head_step(head, carry):
        wait_memory(head)

        @pl.when(head < LOCAL - 2)
        def _():
            send_memory(head + 2)

        wait_in((2, 3), head)

        def shard_step(i, total):
            shard = far(core + 1 + i, 2)
            total = total + attend(head, shard)
            for dt in (2, 1, 3):
                send_out(head, shard, dt, False)

            @pl.when(i == 0)
            def _():
                send_out(head, shard, 0, False)

            @pl.when(i == 1)
            def _():
                send_out(head, shard, 0, True)

            return total

        part_bias[head] = lax.fori_loop(0, 2, shard_step, jnp.zeros((8, HEAD), jnp.float32))

        @pl.when(head < LOCAL - 2)
        def _():
            forward(head + 2)

        return carry

    lax.fori_loop(0, LOCAL, head_step, 0)

    def gather_ring(parts, own, size, ups, up_to, down_to, sends, receives):
        downs = size - 1 - ups
        for step in range(max(ups, downs)):
            incoming = []
            for way, count, device in ((1, ups, up_to), (-1, downs, down_to)):
                if step < count:
                    outgoing = far(own - way * step + size, size)
                    pltpu.make_async_remote_copy(
                        parts.at[outgoing], parts.at[outgoing], sends, receives.at[outgoing],
                        device_id=device, device_id_type=MESH,
                    ).start()
                    incoming.append(far(own - way * (step + 1) + size, size))
            for slot in incoming:
                pltpu.make_async_copy(parts.at[slot], parts.at[slot], receives.at[slot]).wait()
        return jnp.sum(parts[...], axis=0)

    z_bias[z] = jnp.sum(part_bias[...], axis=1)
    pl.semaphore_wait(hello, 1)
    y_bias[y] = gather_ring(z_bias, z, depth, depth // 2, place(z + 1, y), place(z - 1, y), z_sem, z_recv)
    sum_bias[core] = gather_ring(y_bias, y, RING, 1, relay_from, relay_to, y_sem, y_recv)
    swap_bias = pltpu.make_async_remote_copy(
        sum_bias.at[core], sum_bias.at[core], info_sem.at[0], info_sem.at[1],
        device_id=x_peer(1, 0), device_id_type=MESH,
    )
    swap_bias.start()
    swap_bias.wait()
    for which in range(2):
        gb_ref[pl.ds(which * LOCAL, LOCAL), :] = sum_bias[which, 0:LOCAL]

    for which in range(4):
        ref = outputs[which][1]
        pltpu.make_async_copy(ref, ref, out_recv.at[which]).wait()
        part = ref.at[:, pl.ds(0, 7 * LOCAL * HEAD)]
        pltpu.make_async_copy(part, part, out_send.at[which]).wait()
        pltpu.make_async_copy(part, part, in_send.at[which]).wait()
    for which, buf in enumerate((k_buf, v_buf)):
        ref = buf.at[:, pl.ds(0, MEM)]
        pltpu.make_async_copy(ref, ref, mem_send.at[which]).wait()
        relay = (k_relay, v_relay)[which]
        pltpu.make_async_copy(relay, relay, relay_send.at[which]).wait()
    sent = z_bias.at[pl.ds(0, depth - 1)]
    pltpu.make_async_copy(sent, sent, z_sem).wait()
    sent = y_bias.at[pl.ds(0, RING - 1)]
    pltpu.make_async_copy(sent, sent, y_sem).wait()


def write_out(o_in, gq_in, gk_in, gv_in, gb_in, o_ref, gq_ref, gk_ref, gv_ref, gb_ref, sem):
    pairs = ((o_in, o_ref), (gq_in, gq_ref), (gk_in, gk_ref), (gv_in, gv_ref), (gb_in, gb_ref))
    copies = [pltpu.make_async_copy(source, target, sem.at[i]) for i, (source, target) in enumerate(pairs)]
    for copy in copies:
        copy.start()
    for copy in copies:
        copy.wait()


def solution(mesh):
    depth = mesh.shape["ctx"] // (2 * RING)
    half = jnp.bfloat16

    def step(queries, keys, values, cotangent, content_bias, memory_lengths, segment_ends):
        any_spec = pl.BlockSpec(memory_space=pl.ANY)
        vmem_spec = pl.BlockSpec(memory_space=pltpu.VMEM)
        smem_spec = pl.BlockSpec(memory_space=pltpu.SMEM)
        slab = jax.ShapeDtypeStruct(queries.shape, half)
        dma, vmem = pltpu.SemaphoreType.DMA, pltpu.VMEM
        found = pl.pallas_call(
            functools.partial(kernel, depth),
            out_shape=(slab, slab, slab, slab, jax.ShapeDtypeStruct(content_bias.shape, jnp.float32)),
            in_specs=[any_spec] * 4 + [vmem_spec, smem_spec, smem_spec],
            out_specs=[any_spec] * 4 + [vmem_spec],
            scratch_shapes=[
                vmem((LOCAL, 2 * ROWS, HEAD), half),
                vmem((LOCAL, 2 * ROWS, HEAD), half),
                vmem((LOCAL, SPAN, HEAD), half),
                vmem((LOCAL, SPAN, HEAD), half),
                vmem((LOCAL, 2 * ROWS, HEAD), half),
                vmem((LOCAL, 2 * ROWS, HEAD), half),
                vmem((LOCAL, 2 * ROWS, HEAD), half),
                vmem((LOCAL, 2 * ROWS, HEAD), half),
                vmem((LOCAL, ROWS, HEAD), half),
                vmem((LOCAL, ROWS, HEAD), half),
                vmem((2, 8, 128), jnp.float32),
                vmem((2, ROWS, WIDE), jnp.float32),
                vmem((8, 8, HEAD), jnp.float32),
                vmem((depth, 8, HEAD), jnp.float32),
                vmem((RING, 8, HEAD), jnp.float32),
                vmem((2, 8, HEAD), jnp.float32),
                dma((4,)),
                dma((4, LOCAL)),
                dma((2,)),
                dma((2, LOCAL)),
                dma((2,)),
                dma((2, LOCAL)),
                dma((4,)),
                dma((4,)),
                dma((2,)),
                dma(()),
                dma((depth,)),
                dma(()),
                dma((RING,)),
                pltpu.SemaphoreType.REGULAR,
            ],
            compiler_params=pltpu.CompilerParams(
                collective_id=1, has_side_effects=True, vmem_limit_bytes=VLIMIT * 1024 * 1024
            ),
            cost_estimate=pl.CostEstimate(flops=12 * 10**9, bytes_accessed=20 * 10**6, transcendentals=10**7),
        )(queries, keys, values, cotangent, content_bias, memory_lengths, segment_ends)
        return pl.pallas_call(
            write_out,
            out_shape=(slab, slab, slab, slab, jax.ShapeDtypeStruct(content_bias.shape, jnp.float32)),
            in_specs=[any_spec] * 5,
            out_specs=[any_spec] * 5,
            scratch_shapes=[dma((5,))],
            compiler_params=pltpu.CompilerParams(vmem_limit_bytes=16 * 1024 * 1024),
        )(*found)

    tokens = P(("ctx", "tsp"), None)
    return jax.shard_map(
        step,
        mesh=mesh,
        in_specs=(tokens, tokens, tokens, tokens, P("tsp", None), P("ctx"), P("ctx")),
        out_specs=(tokens, tokens, tokens, tokens, P("tsp", None)),
        check_vma=False,
    )
```

```python
import functools
import math

import jax
import jax.numpy as jnp
from jax import lax
from jax.experimental import pallas as pl
from jax.experimental.pallas import tpu as pltpu
from jax.sharding import PartitionSpec as P

MESH = pl.DeviceIdType.MESH
MEM = 1536
ROWS = 512
PART = 128
HEAD = 128
TSP = 4
RING = 4
LOCAL = 5
SPAN = MEM + 2 * ROWS
WIDE = MEM + ROWS
HALF = 256
AHEAD = 2
VLIMIT = 46
MASKED = -1e30
SCALING = 1.0 / math.sqrt(HEAD)
LOG2_SCALING = SCALING * math.log2(math.e)
LAST = (((1,), (1,)), ((), ()))
FIRST = (((0,), (0,)), ((), ()))


def kernel(
    depth,
    q_ref, k_ref, v_ref, g_ref, bias_hbm, length_ref, end_ref,
    o_ref, gq_ref, gk_ref, gv_ref, gb_ref,
    q_buf, g_buf, k_buf, v_buf, o_buf, gq_buf, gk_buf, gv_buf,
    bias_ref, k_relay, v_relay, info, mask, part_bias, z_bias, y_bias, sum_bias,
    in_send, in_recv, mem_send, mem_recv, relay_send, relay_recv, out_send, out_recv, info_sem, z_sem, z_recv, y_sem, y_recv, hello, small_sem,
):
    c, t = lax.axis_index("ctx"), lax.axis_index("tsp")
    shards = depth * RING * 2
    core = lax.rem(c, 2)
    pair = c // 2
    y = lax.rem(pair, RING)
    z = pair // RING

    def far(value, n):
        return lax.rem(value, n)

    def x_peer(dk, dt):
        return (pair * 2 + (core if dk == 0 else 1 - core), far(t + dt, TSP))

    def ctx_peer(step):
        return (far(c + step + shards, shards), t)

    def place(z_at, y_at):
        return ((far(z_at + depth, depth) * RING + far(y_at + RING, RING)) * 2 + core, t)

    relay_to = place(z, y - 1)
    relay_from = place(z, y + 1)
    onward_to = place(z + jnp.where((y == 1) | (y == 2), 1, 0), y - 1)
    onward_from = place(z - jnp.where((y == 0) | (y == 1), 1, 0), y + 1)

    x_peers = [(dk, dt) for dt in (1, 2, 3) for dk in (0, 1)] + [(1, 0)]

    fetch = pltpu.make_async_copy(bias_hbm, bias_ref, small_sem)
    fetch.start()

    barrier = pltpu.get_barrier_semaphore()

    def greet(device):
        pl.semaphore_signal(barrier, inc=1, device_id=device, device_id_type=MESH)

    for dk, dt in x_peers:
        greet(x_peer(dk, dt))
    greet(ctx_peer(-2))
    greet(relay_from)
    greet(onward_from)
    greet(place(z - 1, y))
    pl.semaphore_wait(barrier, 7 + 4)
    pl.semaphore_signal(hello, inc=1, device_id=place(z + 1, y), device_id_type=MESH)

    sources = (k_ref, v_ref, q_ref, g_ref)
    own_rows = pl.ds(pl.multiple_of(t * PART, PART), PART)

    def landing(which, head, shard, rows):
        if which < 2:
            first = MEM + shard * ROWS
            buf = (k_buf, v_buf)[which]
        else:
            first = shard * ROWS
            buf = (q_buf, g_buf)[which - 2]
        return buf.at[head, pl.ds(pl.multiple_of(first + rows, PART), PART)]

    def scatter_in(arrays, head):
        for dk, dt in x_peers + [(0, 0)]:
            device = x_peer(dk, dt)
            to_core = core if dk == 0 else 1 - core
            column = (device[1] * 2 + to_core) * LOCAL + head
            columns = pl.ds(pl.multiple_of(column * HEAD, HEAD), HEAD)
            for which in arrays:
                source = sources[which].at[:, columns]
                target = landing(which, head, core, t * PART)
                if (dk, dt) == (0, 0):
                    pltpu.make_async_copy(source, target, in_recv.at[which, head]).start()
                else:
                    pltpu.make_async_remote_copy(
                        source, target, in_send.at[which], in_recv.at[which, head],
                        device_id=device, device_id_type=MESH,
                    ).start()

    def wait_in(arrays, head):
        for which in arrays:
            if which < 2:
                ref = (k_buf, v_buf)[which].at[head, pl.ds(MEM, 2 * ROWS)]
            else:
                ref = (q_buf, g_buf)[which - 2].at[head]
            pltpu.make_async_copy(ref, ref, in_recv.at[which, head]).wait()

    def send_memory(head):
        for which, buf in enumerate((k_buf, v_buf)):
            pltpu.make_async_remote_copy(
                buf.at[head, pl.ds(MEM, 2 * ROWS)], buf.at[head, pl.ds(ROWS, 2 * ROWS)],
                mem_send.at[which], mem_recv.at[which, head],
                device_id=ctx_peer(2), device_id_type=MESH,
            ).start()
            pltpu.make_async_remote_copy(
                buf.at[head, pl.ds(MEM + ROWS, ROWS)], (k_relay, v_relay)[which].at[head],
                relay_send.at[which], relay_recv.at[which, head],
                device_id=relay_to, device_id_type=MESH,
            ).start()

    def forward(head):
        for which, (relay, buf) in enumerate(((k_relay, k_buf), (v_relay, v_buf))):
            pltpu.make_async_copy(relay.at[head], relay.at[head], relay_recv.at[which, head]).wait()
            pltpu.make_async_remote_copy(
                relay.at[head], buf.at[head, pl.ds(0, ROWS)],
                mem_send.at[which], mem_recv.at[which, head],
                device_id=onward_to, device_id_type=MESH,
            ).start()

    def wait_memory(head):
        for which, buf in enumerate((k_buf, v_buf)):
            ref = buf.at[head, pl.ds(0, MEM)]
            pltpu.make_async_copy(ref, ref, mem_recv.at[which, head]).wait()

    part_bias[...] = jnp.zeros_like(part_bias)

    def first_sends(head, carry):
        scatter_in((0, 1), head)
        return carry

    lax.fori_loop(0, AHEAD, first_sends, 0)

    fetch.wait()

    usable = jnp.minimum(length_ref[0], c * ROWS)
    tile_row = lax.broadcasted_iota(jnp.int32, (8, 128), 0)
    info[core] = jnp.where(tile_row == 0, usable, end_ref[0]).astype(jnp.float32)
    swap = pltpu.make_async_remote_copy(
        info.at[core], info.at[core], info_sem.at[0], info_sem.at[1],
        device_id=x_peer(1, 0), device_id_type=MESH,
    )
    swap.start()
    swap.wait()

    def build_mask(step, carry):
        shard, block = step // (WIDE // 128), lax.rem(step, WIDE // 128)
        limit = info[shard]
        allowed_memory = limit[0:1]
        boundary = limit[1:2]
        row = lax.broadcasted_iota(jnp.int32, (ROWS, 128), 0).astype(jnp.float32)
        col = (lax.broadcasted_iota(jnp.int32, (ROWS, 128), 1) + block * 128).astype(jnp.float32)
        offset = col - float(MEM)
        row_first = jnp.where(row < boundary, 1.0, 0.0)
        col_first = jnp.where(offset < boundary, 1.0, 0.0)
        memory_ok = jnp.where(offset >= 0.0 - allowed_memory, row_first, 0.0)
        local_ok = jnp.where((offset <= row) & (row_first == col_first), 1.0, 0.0)
        ok = jnp.where(offset < 0.0, memory_ok, local_ok)
        mask[shard, :, pl.ds(pl.multiple_of(block * 128, 128), 128)] = jnp.where(ok > 0.5, 0.0, MASKED)
        return carry

    lax.fori_loop(0, 2 * (WIDE // 128), build_mask, 0)

    def gather_step(head, carry):
        wait_in((0, 1), head)

        @pl.when(head < 2)
        def _():
            send_memory(head)

        @pl.when(head < LOCAL - AHEAD)
        def _():
            scatter_in((0, 1), head + AHEAD)

        @pl.when(head >= LOCAL - AHEAD)
        def _():
            scatter_in((2, 3), head - (LOCAL - AHEAD))

        @pl.when((head >= 2) & (head < 4))
        def _():
            forward(head - 2)

        return carry

    lax.fori_loop(0, LOCAL, gather_step, 0)

    def last_sends(head, carry):
        scatter_in((2, 3), head)
        return carry

    lax.fori_loop(AHEAD, LOCAL, last_sends, 0)

    outputs = ((o_buf, o_ref), (gq_buf, gq_ref), (gk_buf, gk_ref), (gv_buf, gv_ref))

    def attend(head, shard):
        bias = bias_ref[pl.ds(core * LOCAL + head, 1), :]
        key_first = pl.multiple_of(shard * ROWS, ROWS)
        bias_total = jnp.zeros((8, HEAD), jnp.float32)
        key_parts, value_parts = [], []
        for half in range(2):
            rows = pl.ds(half * HALF, HALF)
            in_rows = pl.ds(pl.multiple_of(shard * ROWS + half * HALF, HALF), HALF)
            span = MEM + HALF * (half + 1)
            shifted = (q_buf[head, in_rows, :].astype(jnp.float32) + bias).astype(jnp.bfloat16)
            grad_rows = g_buf[head, in_rows, :]
            key_rows = k_buf[head, pl.ds(key_first, span), :]
            value_rows = v_buf[head, pl.ds(key_first, span), :]
            scores = lax.dot_general(shifted, key_rows, LAST, preferred_element_type=jnp.float32)
            scores = scores * LOG2_SCALING + mask[shard, rows, 0:span]
            peak = jnp.max(scores, axis=1, keepdims=True)
            weights = jnp.exp2(scores - peak)
            inverse = 1.0 / jnp.sum(weights, axis=1, keepdims=True)
            probs = weights * inverse
            probs_half = probs.astype(jnp.bfloat16)
            attended = jnp.dot(probs_half, value_rows, preferred_element_type=jnp.float32)
            grad_probs = lax.dot_general(grad_rows, value_rows, LAST, preferred_element_type=jnp.float32)
            centre = jnp.sum(probs * grad_probs, axis=1, keepdims=True)
            grad_scores = (probs * (grad_probs - centre) * SCALING).astype(jnp.bfloat16)
            grad_query = jnp.dot(grad_scores, key_rows, preferred_element_type=jnp.float32)
            out_rows = in_rows
            o_buf[head, out_rows, :] = attended.astype(jnp.bfloat16)
            gq_buf[head, out_rows, :] = grad_query.astype(jnp.bfloat16)
            bias_total += jnp.sum(grad_query.reshape(HALF // 8, 8, HEAD), axis=0)
            key_parts.append(
                lax.dot_general(grad_scores[:, MEM:], shifted, FIRST, preferred_element_type=jnp.float32)
            )
            value_parts.append(
                lax.dot_general(probs_half[:, MEM:], grad_rows, FIRST, preferred_element_type=jnp.float32)
            )
        for buf, parts in ((gk_buf, key_parts), (gv_buf, value_parts)):
            low = pl.ds(pl.multiple_of(shard * ROWS, HALF), HALF)
            high = pl.ds(pl.multiple_of(shard * ROWS + HALF, HALF), HALF)
            buf[head, low, :] = (parts[0] + parts[1][:HALF]).astype(jnp.bfloat16)
            buf[head, high, :] = parts[1][HALF:].astype(jnp.bfloat16)
        return bias_total

    def send_out(head, shard, dt, local):
        to_part = far(t + dt, TSP)
        column = (t * 2 + core) * LOCAL + head
        columns = pl.ds(pl.multiple_of(column * HEAD, HEAD), HEAD)
        rows = pl.ds(pl.multiple_of(shard * ROWS + to_part * PART, PART), PART)
        for which, (buf, ref) in enumerate(outputs):
            source, target = buf.at[head, rows], ref.at[:, columns]
            if local:
                pltpu.make_async_copy(source, target, out_recv.at[which]).start()
            else:
                pltpu.make_async_remote_copy(
                    source, target, out_send.at[which], out_recv.at[which],
                    device_id=(pair * 2 + shard, to_part), device_id_type=MESH,
                ).start()

    def head_step(head, carry):
        wait_memory(head)

        @pl.when(head < LOCAL - 2)
        def _():
            send_memory(head + 2)

        wait_in((2, 3), head)

        def shard_step(i, total):
            shard = far(core + 1 + i, 2)
            total = total + attend(head, shard)
            for dt in (2, 1, 3):
                send_out(head, shard, dt, False)

            @pl.when(i == 0)
            def _():
                send_out(head, shard, 0, False)

            @pl.when(i == 1)
            def _():
                send_out(head, shard, 0, True)

            return total

        part_bias[head] = lax.fori_loop(0, 2, shard_step, jnp.zeros((8, HEAD), jnp.float32))

        @pl.when(head < LOCAL - 2)
        def _():
            forward(head + 2)

        return carry

    lax.fori_loop(0, LOCAL, head_step, 0)

    def gather_ring(parts, own, size, ups, up_to, down_to, sends, receives):
        downs = size - 1 - ups
        for step in range(max(ups, downs)):
            incoming = []
            for way, count, device in ((1, ups, up_to), (-1, downs, down_to)):
                if step < count:
                    outgoing = far(own - way * step + size, size)
                    pltpu.make_async_remote_copy(
                        parts.at[outgoing], parts.at[outgoing], sends, receives.at[outgoing],
                        device_id=device, device_id_type=MESH,
                    ).start()
                    incoming.append(far(own - way * (step + 1) + size, size))
            for slot in incoming:
                pltpu.make_async_copy(parts.at[slot], parts.at[slot], receives.at[slot]).wait()
        return jnp.sum(parts[...], axis=0)

    z_bias[z] = jnp.sum(part_bias[...], axis=1)
    pl.semaphore_wait(hello, 1)
    y_bias[y] = gather_ring(z_bias, z, depth, depth // 2, place(z + 1, y), place(z - 1, y), z_sem, z_recv)
    sum_bias[core] = gather_ring(y_bias, y, RING, 1, relay_from, relay_to, y_sem, y_recv)
    swap_bias = pltpu.make_async_remote_copy(
        sum_bias.at[core], sum_bias.at[core], info_sem.at[0], info_sem.at[1],
        device_id=x_peer(1, 0), device_id_type=MESH,
    )
    swap_bias.start()
    swap_bias.wait()
    for which in range(2):
        gb_ref[pl.ds(which * LOCAL, LOCAL), :] = sum_bias[which, 0:LOCAL]

    for which in range(4):
        ref = outputs[which][1]
        pltpu.make_async_copy(ref, ref, out_recv.at[which]).wait()
        part = ref.at[:, pl.ds(0, 7 * LOCAL * HEAD)]
        pltpu.make_async_copy(part, part, out_send.at[which]).wait()
        pltpu.make_async_copy(part, part, in_send.at[which]).wait()
    for which, buf in enumerate((k_buf, v_buf)):
        ref = buf.at[:, pl.ds(0, MEM)]
        pltpu.make_async_copy(ref, ref, mem_send.at[which]).wait()
        relay = (k_relay, v_relay)[which]
        pltpu.make_async_copy(relay, relay, relay_send.at[which]).wait()
    sent = z_bias.at[pl.ds(0, depth - 1)]
    pltpu.make_async_copy(sent, sent, z_sem).wait()
    sent = y_bias.at[pl.ds(0, RING - 1)]
    pltpu.make_async_copy(sent, sent, y_sem).wait()


def write_out(o_in, gq_in, gk_in, gv_in, gb_in, o_ref, gq_ref, gk_ref, gv_ref, gb_ref, sem):
    pairs = ((o_in, o_ref), (gq_in, gq_ref), (gk_in, gk_ref), (gv_in, gv_ref), (gb_in, gb_ref))
    copies = [pltpu.make_async_copy(source, target, sem.at[i]) for i, (source, target) in enumerate(pairs)]
    for copy in copies:
        copy.start()
    for copy in copies:
        copy.wait()


def solution(mesh):
    depth = mesh.shape["ctx"] // (2 * RING)
    half = jnp.bfloat16

    def step(queries, keys, values, cotangent, content_bias, memory_lengths, segment_ends):
        any_spec = pl.BlockSpec(memory_space=pl.ANY)
        smem_spec = pl.BlockSpec(memory_space=pltpu.SMEM)
        vmem_spec = pl.BlockSpec(memory_space=pltpu.VMEM)
        slab = jax.ShapeDtypeStruct(queries.shape, half)
        dma, vmem = pltpu.SemaphoreType.DMA, pltpu.VMEM
        in_hbm = [
            pltpu.with_memory_space_constraint(value, pltpu.HBM)
            for value in (queries, keys, values, cotangent, content_bias)
        ]
        found = pl.pallas_call(
            functools.partial(kernel, depth),
            out_shape=[vmem(queries.shape, half)] * 4 + [vmem(content_bias.shape, jnp.float32)],
            in_specs=[pl.BlockSpec(memory_space=pltpu.HBM)] * 5 + [smem_spec, smem_spec],
            out_specs=[vmem_spec] * 5,
            scratch_shapes=[
                vmem((LOCAL, 2 * ROWS, HEAD), half),
                vmem((LOCAL, 2 * ROWS, HEAD), half),
                vmem((LOCAL, SPAN, HEAD), half),
                vmem((LOCAL, SPAN, HEAD), half),
                vmem((LOCAL, 2 * ROWS, HEAD), half),
                vmem((LOCAL, 2 * ROWS, HEAD), half),
                vmem((LOCAL, 2 * ROWS, HEAD), half),
                vmem((LOCAL, 2 * ROWS, HEAD), half),
                vmem(content_bias.shape, jnp.float32),
                vmem((LOCAL, ROWS, HEAD), half),
                vmem((LOCAL, ROWS, HEAD), half),
                vmem((2, 8, 128), jnp.float32),
                vmem((2, ROWS, WIDE), jnp.float32),
                vmem((8, 8, HEAD), jnp.float32),
                vmem((depth, 8, HEAD), jnp.float32),
                vmem((RING, 8, HEAD), jnp.float32),
                vmem((2, 8, HEAD), jnp.float32),
                dma((4,)),
                dma((4, LOCAL)),
                dma((2,)),
                dma((2, LOCAL)),
                dma((2,)),
                dma((2, LOCAL)),
                dma((4,)),
                dma((4,)),
                dma((2,)),
                dma(()),
                dma((depth,)),
                dma(()),
                dma((RING,)),
                pltpu.SemaphoreType.REGULAR,
                dma(()),
            ],
            compiler_params=pltpu.CompilerParams(
                collective_id=1, has_side_effects=True, vmem_limit_bytes=VLIMIT * 1024 * 1024
            ),
            cost_estimate=pl.CostEstimate(flops=12 * 10**9, bytes_accessed=20 * 10**6, transcendentals=10**7),
        )(*in_hbm, memory_lengths, segment_ends)
        return pl.pallas_call(
            write_out,
            out_shape=(slab, slab, slab, slab, jax.ShapeDtypeStruct(content_bias.shape, jnp.float32)),
            in_specs=[any_spec] * 5,
            out_specs=[any_spec] * 5,
            scratch_shapes=[dma((5,))],
            compiler_params=pltpu.CompilerParams(vmem_limit_bytes=16 * 1024 * 1024),
        )(*found)

    tokens = P(("ctx", "tsp"), None)
    return jax.shard_map(
        step,
        mesh=mesh,
        in_specs=(tokens, tokens, tokens, tokens, P("tsp", None), P("ctx"), P("ctx")),
        out_specs=(tokens, tokens, tokens, tokens, P("tsp", None)),
        check_vma=False,
    )
```

```python
import functools
import math

import jax
import jax.numpy as jnp
from jax import lax
from jax.experimental import pallas as pl
from jax.experimental.pallas import tpu as pltpu
from jax.sharding import PartitionSpec as P

MESH = pl.DeviceIdType.MESH
MEM = 1536
ROWS = 512
PART = 128
HEAD = 128
TSP = 4
RING = 4
LOCAL = 5
SPAN = MEM + 2 * ROWS
WIDE = MEM + ROWS
HALF = 256
AHEAD = 2
VLIMIT = 46
MASKED = -1e30
SCALING = 1.0 / math.sqrt(HEAD)
LOG2_SCALING = SCALING * math.log2(math.e)
LAST = (((1,), (1,)), ((), ()))
FIRST = (((0,), (0,)), ((), ()))


def kernel(
    depth,
    q_ref, k_ref, v_ref, g_ref, bias_hbm, length_ref, end_ref,
    o_ref, gq_ref, gk_ref, gv_ref, gb_ref,
    q_buf, g_buf, k_buf, v_buf, o_buf, gq_buf, gk_buf, gv_buf,
    bias_ref, k_relay, v_relay, info, mask, part_bias, z_bias, y_bias, sum_bias,
    in_send, in_recv, mem_send, mem_recv, relay_send, relay_recv, out_send, out_recv, info_sem, z_sem, z_recv, y_sem, y_recv, hello, small_sem,
):
    c, t = lax.axis_index("ctx"), lax.axis_index("tsp")
    shards = depth * RING * 2
    core = lax.rem(c, 2)
    pair = c // 2
    y = lax.rem(pair, RING)
    z = pair // RING

    def far(value, n):
        return lax.rem(value, n)

    def x_peer(dk, dt):
        return (pair * 2 + (core if dk == 0 else 1 - core), far(t + dt, TSP))

    def ctx_peer(step):
        return (far(c + step + shards, shards), t)

    def place(z_at, y_at):
        return ((far(z_at + depth, depth) * RING + far(y_at + RING, RING)) * 2 + core, t)

    relay_to = place(z, y - 1)
    relay_from = place(z, y + 1)
    onward_to = place(z + jnp.where((y == 1) | (y == 2), 1, 0), y - 1)
    onward_from = place(z - jnp.where((y == 0) | (y == 1), 1, 0), y + 1)

    x_peers = [(dk, dt) for dt in (1, 2, 3) for dk in (0, 1)] + [(1, 0)]

    fetch = pltpu.make_async_copy(bias_hbm, bias_ref, small_sem)
    fetch.start()

    barrier = pltpu.get_barrier_semaphore()

    def greet(device):
        pl.semaphore_signal(barrier, inc=1, device_id=device, device_id_type=MESH)

    for dk, dt in x_peers:
        greet(x_peer(dk, dt))
    greet(ctx_peer(-2))
    greet(relay_from)
    greet(onward_from)
    greet(place(z - 1, y))
    pl.semaphore_wait(barrier, 7 + 4)
    pl.semaphore_signal(hello, inc=1, device_id=place(z + 1, y), device_id_type=MESH)

    sources = (k_ref, v_ref, q_ref, g_ref)
    own_rows = pl.ds(pl.multiple_of(t * PART, PART), PART)

    def landing(which, head, shard, rows):
        if which < 2:
            first = MEM + shard * ROWS
            buf = (k_buf, v_buf)[which]
        else:
            first = shard * ROWS
            buf = (q_buf, g_buf)[which - 2]
        return buf.at[head, pl.ds(pl.multiple_of(first + rows, PART), PART)]

    def scatter_in(arrays, head):
        for dk, dt in x_peers + [(0, 0)]:
            device = x_peer(dk, dt)
            to_core = core if dk == 0 else 1 - core
            column = (device[1] * 2 + to_core) * LOCAL + head
            columns = pl.ds(pl.multiple_of(column * HEAD, HEAD), HEAD)
            for which in arrays:
                source = sources[which].at[:, columns]
                target = landing(which, head, core, t * PART)
                if (dk, dt) == (0, 0):
                    pltpu.make_async_copy(source, target, in_recv.at[which, head]).start()
                else:
                    pltpu.make_async_remote_copy(
                        source, target, in_send.at[which], in_recv.at[which, head],
                        device_id=device, device_id_type=MESH,
                    ).start()

    def wait_in(arrays, head):
        for which in arrays:
            if which < 2:
                ref = (k_buf, v_buf)[which].at[head, pl.ds(MEM, 2 * ROWS)]
            else:
                ref = (q_buf, g_buf)[which - 2].at[head]
            pltpu.make_async_copy(ref, ref, in_recv.at[which, head]).wait()

    def send_memory(head):
        for which, buf in enumerate((k_buf, v_buf)):
            pltpu.make_async_remote_copy(
                buf.at[head, pl.ds(MEM, 2 * ROWS)], buf.at[head, pl.ds(ROWS, 2 * ROWS)],
                mem_send.at[which], mem_recv.at[which, head],
                device_id=ctx_peer(2), device_id_type=MESH,
            ).start()
            pltpu.make_async_remote_copy(
                buf.at[head, pl.ds(MEM + ROWS, ROWS)], (k_relay, v_relay)[which].at[head],
                relay_send.at[which], relay_recv.at[which, head],
                device_id=relay_to, device_id_type=MESH,
            ).start()

    def forward(head):
        for which, (relay, buf) in enumerate(((k_relay, k_buf), (v_relay, v_buf))):
            pltpu.make_async_copy(relay.at[head], relay.at[head], relay_recv.at[which, head]).wait()
            pltpu.make_async_remote_copy(
                relay.at[head], buf.at[head, pl.ds(0, ROWS)],
                mem_send.at[which], mem_recv.at[which, head],
                device_id=onward_to, device_id_type=MESH,
            ).start()

    def wait_memory(head):
        for which, buf in enumerate((k_buf, v_buf)):
            ref = buf.at[head, pl.ds(0, MEM)]
            pltpu.make_async_copy(ref, ref, mem_recv.at[which, head]).wait()

    part_bias[...] = jnp.zeros_like(part_bias)

    def first_sends(head, carry):
        scatter_in((0, 1), head)
        return carry

    lax.fori_loop(0, AHEAD, first_sends, 0)

    fetch.wait()

    usable = jnp.minimum(length_ref[0], c * ROWS)
    tile_row = lax.broadcasted_iota(jnp.int32, (8, 128), 0)
    info[core] = jnp.where(tile_row == 0, usable, end_ref[0]).astype(jnp.float32)
    swap = pltpu.make_async_remote_copy(
        info.at[core], info.at[core], info_sem.at[0], info_sem.at[1],
        device_id=x_peer(1, 0), device_id_type=MESH,
    )
    swap.start()
    swap.wait()

    def build_mask(step, carry):
        shard, block = step // (WIDE // 128), lax.rem(step, WIDE // 128)
        limit = info[shard]
        allowed_memory = limit[0:1]
        boundary = limit[1:2]
        row = lax.broadcasted_iota(jnp.int32, (ROWS, 128), 0).astype(jnp.float32)
        col = (lax.broadcasted_iota(jnp.int32, (ROWS, 128), 1) + block * 128).astype(jnp.float32)
        offset = col - float(MEM)
        row_first = jnp.where(row < boundary, 1.0, 0.0)
        col_first = jnp.where(offset < boundary, 1.0, 0.0)
        memory_ok = jnp.where(offset >= 0.0 - allowed_memory, row_first, 0.0)
        local_ok = jnp.where((offset <= row) & (row_first == col_first), 1.0, 0.0)
        ok = jnp.where(offset < 0.0, memory_ok, local_ok)
        mask[shard, :, pl.ds(pl.multiple_of(block * 128, 128), 128)] = jnp.where(ok > 0.5, 0.0, MASKED)
        return carry

    lax.fori_loop(0, 2 * (WIDE // 128), build_mask, 0)

    def gather_step(head, carry):
        wait_in((0, 1), head)

        @pl.when(head < 3)
        def _():
            send_memory(head)

        @pl.when(head < LOCAL - AHEAD)
        def _():
            scatter_in((0, 1), head + AHEAD)

        @pl.when(head >= LOCAL - AHEAD)
        def _():
            scatter_in((2, 3), head - (LOCAL - AHEAD))

        @pl.when((head >= 2) & (head < 4))
        def _():
            forward(head - 2)

        return carry

    lax.fori_loop(0, LOCAL, gather_step, 0)

    def last_sends(head, carry):
        scatter_in((2, 3), head)
        return carry

    lax.fori_loop(AHEAD, LOCAL, last_sends, 0)

    outputs = ((o_buf, o_ref), (gq_buf, gq_ref), (gk_buf, gk_ref), (gv_buf, gv_ref))

    def attend(head, shard):
        bias = bias_ref[pl.ds(core * LOCAL + head, 1), :]
        key_first = pl.multiple_of(shard * ROWS, ROWS)
        bias_total = jnp.zeros((8, HEAD), jnp.float32)
        key_parts, value_parts = [], []
        for half in range(2):
            rows = pl.ds(half * HALF, HALF)
            in_rows = pl.ds(pl.multiple_of(shard * ROWS + half * HALF, HALF), HALF)
            span = MEM + HALF * (half + 1)
            shifted = (q_buf[head, in_rows, :].astype(jnp.float32) + bias).astype(jnp.bfloat16)
            grad_rows = g_buf[head, in_rows, :]
            key_rows = k_buf[head, pl.ds(key_first, span), :]
            value_rows = v_buf[head, pl.ds(key_first, span), :]
            scores = lax.dot_general(shifted, key_rows, LAST, preferred_element_type=jnp.float32)
            scores = scores * LOG2_SCALING + mask[shard, rows, 0:span]
            peak = jnp.max(scores, axis=1, keepdims=True)
            weights = jnp.exp2(scores - peak)
            inverse = 1.0 / jnp.sum(weights, axis=1, keepdims=True)
            probs = weights * inverse
            probs_half = probs.astype(jnp.bfloat16)
            attended = jnp.dot(probs_half, value_rows, preferred_element_type=jnp.float32)
            grad_probs = lax.dot_general(grad_rows, value_rows, LAST, preferred_element_type=jnp.float32)
            centre = jnp.sum(probs * grad_probs, axis=1, keepdims=True)
            grad_scores = (probs * (grad_probs - centre) * SCALING).astype(jnp.bfloat16)
            grad_query = jnp.dot(grad_scores, key_rows, preferred_element_type=jnp.float32)
            out_rows = in_rows
            o_buf[head, out_rows, :] = attended.astype(jnp.bfloat16)
            gq_buf[head, out_rows, :] = grad_query.astype(jnp.bfloat16)
            bias_total += jnp.sum(grad_query.reshape(HALF // 8, 8, HEAD), axis=0)
            key_parts.append(
                lax.dot_general(grad_scores[:, MEM:], shifted, FIRST, preferred_element_type=jnp.float32)
            )
            value_parts.append(
                lax.dot_general(probs_half[:, MEM:], grad_rows, FIRST, preferred_element_type=jnp.float32)
            )
        for buf, parts in ((gk_buf, key_parts), (gv_buf, value_parts)):
            low = pl.ds(pl.multiple_of(shard * ROWS, HALF), HALF)
            high = pl.ds(pl.multiple_of(shard * ROWS + HALF, HALF), HALF)
            buf[head, low, :] = (parts[0] + parts[1][:HALF]).astype(jnp.bfloat16)
            buf[head, high, :] = parts[1][HALF:].astype(jnp.bfloat16)
        return bias_total

    def send_out(head, shard, dt, local):
        to_part = far(t + dt, TSP)
        column = (t * 2 + core) * LOCAL + head
        columns = pl.ds(pl.multiple_of(column * HEAD, HEAD), HEAD)
        rows = pl.ds(pl.multiple_of(shard * ROWS + to_part * PART, PART), PART)
        for which, (buf, ref) in enumerate(outputs):
            source, target = buf.at[head, rows], ref.at[:, columns]
            if local:
                pltpu.make_async_copy(source, target, out_recv.at[which]).start()
            else:
                pltpu.make_async_remote_copy(
                    source, target, out_send.at[which], out_recv.at[which],
                    device_id=(pair * 2 + shard, to_part), device_id_type=MESH,
                ).start()

    def head_step(head, carry):
        wait_memory(head)

        @pl.when(head < LOCAL - 3)
        def _():
            send_memory(head + 3)

        wait_in((2, 3), head)

        def shard_step(i, total):
            shard = far(core + 1 + i, 2)
            total = total + attend(head, shard)
            for dt in (2, 1, 3):
                send_out(head, shard, dt, False)

            @pl.when(i == 0)
            def _():
                send_out(head, shard, 0, False)

            @pl.when(i == 1)
            def _():
                send_out(head, shard, 0, True)

            return total

        part_bias[head] = lax.fori_loop(0, 2, shard_step, jnp.zeros((8, HEAD), jnp.float32))

        @pl.when(head < LOCAL - 2)
        def _():
            forward(head + 2)

        return carry

    lax.fori_loop(0, LOCAL, head_step, 0)

    def gather_ring(parts, own, size, ups, up_to, down_to, sends, receives):
        downs = size - 1 - ups
        for step in range(max(ups, downs)):
            incoming = []
            for way, count, device in ((1, ups, up_to), (-1, downs, down_to)):
                if step < count:
                    outgoing = far(own - way * step + size, size)
                    pltpu.make_async_remote_copy(
                        parts.at[outgoing], parts.at[outgoing], sends, receives.at[outgoing],
                        device_id=device, device_id_type=MESH,
                    ).start()
                    incoming.append(far(own - way * (step + 1) + size, size))
            for slot in incoming:
                pltpu.make_async_copy(parts.at[slot], parts.at[slot], receives.at[slot]).wait()
        return jnp.sum(parts[...], axis=0)

    z_bias[z] = jnp.sum(part_bias[...], axis=1)
    pl.semaphore_wait(hello, 1)
    y_bias[y] = gather_ring(z_bias, z, depth, depth // 2, place(z + 1, y), place(z - 1, y), z_sem, z_recv)
    sum_bias[core] = gather_ring(y_bias, y, RING, 1, relay_from, relay_to, y_sem, y_recv)
    swap_bias = pltpu.make_async_remote_copy(
        sum_bias.at[core], sum_bias.at[core], info_sem.at[0], info_sem.at[1],
        device_id=x_peer(1, 0), device_id_type=MESH,
    )
    swap_bias.start()
    swap_bias.wait()
    for which in range(2):
        gb_ref[pl.ds(which * LOCAL, LOCAL), :] = sum_bias[which, 0:LOCAL]

    for which in range(4):
        ref = outputs[which][1]
        pltpu.make_async_copy(ref, ref, out_recv.at[which]).wait()
        part = ref.at[:, pl.ds(0, 7 * LOCAL * HEAD)]
        pltpu.make_async_copy(part, part, out_send.at[which]).wait()
        pltpu.make_async_copy(part, part, in_send.at[which]).wait()
    for which, buf in enumerate((k_buf, v_buf)):
        ref = buf.at[:, pl.ds(0, MEM)]
        pltpu.make_async_copy(ref, ref, mem_send.at[which]).wait()
        relay = (k_relay, v_relay)[which]
        pltpu.make_async_copy(relay, relay, relay_send.at[which]).wait()
    sent = z_bias.at[pl.ds(0, depth - 1)]
    pltpu.make_async_copy(sent, sent, z_sem).wait()
    sent = y_bias.at[pl.ds(0, RING - 1)]
    pltpu.make_async_copy(sent, sent, y_sem).wait()


def write_out(o_in, gq_in, gk_in, gv_in, gb_in, o_ref, gq_ref, gk_ref, gv_ref, gb_ref, sem):
    pairs = ((o_in, o_ref), (gq_in, gq_ref), (gk_in, gk_ref), (gv_in, gv_ref), (gb_in, gb_ref))
    copies = [pltpu.make_async_copy(source, target, sem.at[i]) for i, (source, target) in enumerate(pairs)]
    for copy in copies:
        copy.start()
    for copy in copies:
        copy.wait()


def solution(mesh):
    depth = mesh.shape["ctx"] // (2 * RING)
    half = jnp.bfloat16

    def step(queries, keys, values, cotangent, content_bias, memory_lengths, segment_ends):
        any_spec = pl.BlockSpec(memory_space=pl.ANY)
        smem_spec = pl.BlockSpec(memory_space=pltpu.SMEM)
        vmem_spec = pl.BlockSpec(memory_space=pltpu.VMEM)
        slab = jax.ShapeDtypeStruct(queries.shape, half)
        dma, vmem = pltpu.SemaphoreType.DMA, pltpu.VMEM
        in_hbm = [
            pltpu.with_memory_space_constraint(value, pltpu.HBM)
            for value in (queries, keys, values, cotangent, content_bias)
        ]
        found = pl.pallas_call(
            functools.partial(kernel, depth),
            out_shape=[vmem(queries.shape, half)] * 4 + [vmem(content_bias.shape, jnp.float32)],
            in_specs=[pl.BlockSpec(memory_space=pltpu.HBM)] * 5 + [smem_spec, smem_spec],
            out_specs=[vmem_spec] * 5,
            scratch_shapes=[
                vmem((LOCAL, 2 * ROWS, HEAD), half),
                vmem((LOCAL, 2 * ROWS, HEAD), half),
                vmem((LOCAL, SPAN, HEAD), half),
                vmem((LOCAL, SPAN, HEAD), half),
                vmem((LOCAL, 2 * ROWS, HEAD), half),
                vmem((LOCAL, 2 * ROWS, HEAD), half),
                vmem((LOCAL, 2 * ROWS, HEAD), half),
                vmem((LOCAL, 2 * ROWS, HEAD), half),
                vmem(content_bias.shape, jnp.float32),
                vmem((LOCAL, ROWS, HEAD), half),
                vmem((LOCAL, ROWS, HEAD), half),
                vmem((2, 8, 128), jnp.float32),
                vmem((2, ROWS, WIDE), jnp.float32),
                vmem((8, 8, HEAD), jnp.float32),
                vmem((depth, 8, HEAD), jnp.float32),
                vmem((RING, 8, HEAD), jnp.float32),
                vmem((2, 8, HEAD), jnp.float32),
                dma((4,)),
                dma((4, LOCAL)),
                dma((2,)),
                dma((2, LOCAL)),
                dma((2,)),
                dma((2, LOCAL)),
                dma((4,)),
                dma((4,)),
                dma((2,)),
                dma(()),
                dma((depth,)),
                dma(()),
                dma((RING,)),
                pltpu.SemaphoreType.REGULAR,
                dma(()),
            ],
            compiler_params=pltpu.CompilerParams(
                collective_id=1, has_side_effects=True, vmem_limit_bytes=VLIMIT * 1024 * 1024
            ),
            cost_estimate=pl.CostEstimate(flops=12 * 10**9, bytes_accessed=20 * 10**6, transcendentals=10**7),
        )(*in_hbm, memory_lengths, segment_ends)
        return pl.pallas_call(
            write_out,
            out_shape=(slab, slab, slab, slab, jax.ShapeDtypeStruct(content_bias.shape, jnp.float32)),
            in_specs=[any_spec] * 5,
            out_specs=[any_spec] * 5,
            scratch_shapes=[dma((5,))],
            compiler_params=pltpu.CompilerParams(vmem_limit_bytes=16 * 1024 * 1024),
        )(*found)

    tokens = P(("ctx", "tsp"), None)
    return jax.shard_map(
        step,
        mesh=mesh,
        in_specs=(tokens, tokens, tokens, tokens, P("tsp", None), P("ctx"), P("ctx")),
        out_specs=(tokens, tokens, tokens, tokens, P("tsp", None)),
        check_vma=False,
    )
```
